512 devices in a mesh: tile: 64 (over z_hi, x, y), mem: 8 (over z_lo, core).
Axes of the slice: x: 4, y: 4, z: 16 (z_hi: 4, z_lo: 4; z = z_hi * 4 + z_lo), core: 2. Of those that a mesh axis runs over, the one named last changes fastest.
Arguments:
- control: float32 [64, 32, 16384], P('mem', None, 'tile'), may hold values from -13.5 to 13.5
- perts: bfloat16 [64, 32, 16384], P('mem', None, 'tile'), may hold values from -6 to 6
- diffusivity: float32 [32], replicated, may hold values from 0.08 to 0.245
- vertical: float32 [32, 32], replicated, may hold values from -1 to 1
- gain: float32 [32, 16384], P(None, 'tile'), may hold values from 0.25 to 1.75
- edge_flip: int32 [64, 4], P('tile'), may hold values from 0 to 1, as said below
Outputs:
- increment: float32 [32, 16384], P('mem', 'tile')
- member_cost: float32 [64], P('mem')
The draws below stay inside these ranges and needn't reach their ends.
Inputs may be any that keep to these rules, and one draw needn't show every extreme that they name: edge_flip[t, e] is 1 where the ghost strip beyond edge e of tile t runs in reverse order; both edges of a glued pair carry the same flag.
All inputs are finite; a program needn't handle non-finite values.
Results may differ from the reference program's by a relative error of at most 0.0004.
Values sent between devices are 32-bit elements; how exact they have to be, the bound alone decides.
No kernel may reach another device: no remote copies, remote signals or barrier semaphores. Data moves between devices by JAX's collectives and lax.ppermute only.
A program may use at most 64 MiB of HBM per device.

```python
import math
import jax
import jax.numpy as jnp
from jax import lax

SIDE = 16
CELLS = 256
LEVELS = 32
PASSES = 3
TILES = 64
MEMBERS = 64


def draw_control(key, part):
    key = jax.random.fold_in(key, 3)
    tile_pos = (jnp.arange(TILES * CELLS) // CELLS).astype(jnp.float32)
    scales = jnp.power(3.0, tile_pos / (TILES - 1))
    shape = (MEMBERS, LEVELS, TILES * CELLS)
    base_draw = jax.random.truncated_normal(key, -4.0, 4.0, shape, jnp.float32)
    return (base_draw * scales[None, None, :]).astype(jnp.float32)


def draw_edge_flip(key, part):
    key = jax.random.fold_in(key, 7)
    first_key, second_key = jax.random.split(key)
    ew_bits = jax.random.randint(first_key, (TILES,), 0, 2)
    ns_bits = jax.random.randint(second_key, (TILES,), 0, 2)
    tile_ids = jnp.arange(TILES)
    south_flag = ns_bits[(tile_ids + TILES // 2) % TILES]
    west_flag = ew_bits[(tile_ids + TILES - 1) % TILES]
    return jnp.stack([south_flag, ew_bits, ns_bits, west_flag], axis=1).astype(jnp.int32)


def levels(own_key, shape, shards, smallest, high):
    def one(dim, blocks):
        steps = jax.random.uniform(jax.random.fold_in(jax.random.fold_in(own_key, 6), dim), (blocks,), jnp.float32, smallest / len(shards), high / len(shards))
        return jnp.repeat(jnp.exp(steps), shape[dim] // blocks).reshape((-1,) + (1,) * (len(shape) - dim - 1))

    level = one(*shards[0])
    for cut in shards[1:]:
        level = level * one(*cut)
    return level


def gaussian(stream_key, dims, deviation, limit, cuts=(), kind=jnp.bfloat16):
    result = jax.random.normal(stream_key, dims, jnp.float32) * deviation
    if len(cuts) > 0:
        result = levels(stream_key, dims, cuts, -0.22, 0.18) * result
    return jnp.clip(result, min=-limit, max=limit).astype(kind)


def setup_inputs(seed: int = 0) -> dict:
    keys = jax.random.split(jax.random.key(seed), 7)
    return {
        "control": draw_control(jax.random.fold_in(keys[6], 71), 0),
        "perts": gaussian(keys[1], (MEMBERS, LEVELS, TILES * CELLS), 1.0, 6.0, ((0, 8), (2, 64))),
        "diffusivity": jnp.clip(jnp.exp(jax.random.uniform(keys[2], (LEVELS,), jnp.float32, math.log(0.08), math.log(0.245))), 0.08, 0.245),
        "vertical": gaussian(keys[3], (LEVELS, LEVELS), LEVELS ** -0.5, 1.0, (), jnp.float32),
        "gain": jnp.clip(1.0 + 0.15 * jax.random.normal(keys[4], (LEVELS, TILES * CELLS), jnp.float32), 0.25, 1.75),
        "edge_flip": draw_edge_flip(jax.random.fold_in(keys[6], 71), 0),
    }


def orient(edge_strip, edge_flag):
    return jnp.where(edge_flag[None, :, None] == 1, edge_strip[..., ::-1], edge_strip)

def neighbour_sum(tile_grid, edge_flip):
    tile_ids = jnp.arange(TILES)
    partner = (tile_ids + TILES // 2) % TILES
    next_tile = (tile_ids + 1) % TILES
    prev_tile = (tile_ids + TILES - 1) % TILES
    south_row = tile_grid[:, :, 0, :]
    north_row = tile_grid[:, :, SIDE - 1, :]
    west_col = tile_grid[:, :, :, 0]
    east_col = tile_grid[:, :, :, SIDE - 1]
    h_south = orient(north_row[:, partner], edge_flip[:, 0])
    h_east = orient(west_col[:, next_tile], edge_flip[:, 1])
    h_north = orient(south_row[:, partner], edge_flip[:, 2])
    h_west = orient(east_col[:, prev_tile], edge_flip[:, 3])
    from_above = jnp.concatenate([tile_grid[:, :, 1:, :], h_north[:, :, None, :]], axis=2)
    from_below = jnp.concatenate([h_south[:, :, None, :], tile_grid[:, :, :-1, :]], axis=2)
    from_right = jnp.concatenate([tile_grid[:, :, :, 1:], h_east[:, :, :, None]], axis=3)
    from_left = jnp.concatenate([h_west[:, :, :, None], tile_grid[:, :, :, :-1]], axis=3)
    return from_above + from_below + from_right + from_left

def reference(control, perts, diffusivity, vertical, gain, edge_flip):

    def add_member(running, member_pair):
        field, member_pert = member_pair
        tile_grid = field.reshape(LEVELS, TILES, SIDE, SIDE)
        for repeat in range(PASSES):
            tile_grid = tile_grid + diffusivity[:, None, None, None] * (neighbour_sum(tile_grid, edge_flip) - 4.0 * tile_grid)
        vertical_mix = jnp.dot(vertical, tile_grid.reshape(LEVELS, TILES * CELLS), precision=lax.Precision.HIGHEST)
        return (running + member_pert.astype(jnp.float32) * (gain * vertical_mix), None)
    start = jnp.zeros((LEVELS, TILES * CELLS), jnp.float32)
    running, unused = lax.scan(add_member, start, (control, perts))
    increment = running / jnp.sqrt(jnp.float32(MEMBERS - 1))
    member_cost = 0.5 * lax.optimization_barrier(jnp.sum(control * control, axis=(1, 2))) / (LEVELS * TILES * CELLS)
    return (increment, member_cost)
```

```python
import math

import jax
import jax.numpy as jnp
import numpy as np
from jax import lax
from jax.sharding import PartitionSpec as P

PASSES = 3
SIDE = 16
CELLS = SIDE * SIDE
CORNER = ((0, 0), (0, 1), (1, 0))
LAST = SIDE - 1

EW_ROWS = 64
NS_ROWS = 128
S_, E_, N_, W_ = range(4)


def cell(row, col):
    return row * SIDE + col


def walk_operators():
    names = [("own", i, j) for i in range(SIDE) for j in range(SIDE)]
    for side in "EWNS":
        names += [(side, a, i) for a in range(PASSES) for i in range(SIDE)]
    ends = ("EN", "ES", "WN", "WS", "NE", "NW", "SE", "SW")
    for end in ends:
        names += [(end, a, b) for a, b in CORNER]
    names += [("q", end) for end in ends]
    place = {name: k for k, name in enumerate(names)}
    size = len(names)
    lap = np.zeros((size, size), np.int64)

    def link(name, others):
        row = place[name]
        lap[row, row] -= 4
        for other in others:
            lap[row, place[other]] += 1

    def inside(i, j):
        if i < 0:
            return ("S", -1 - i, j)
        if i > LAST:
            return ("N", i - SIDE, j)
        if j < 0:
            return ("W", -1 - j, i)
        if j > LAST:
            return ("E", j - SIDE, i)
        return ("own", i, j)

    for i in range(SIDE):
        for j in range(SIDE):
            link(("own", i, j), [inside(i + 1, j), inside(i - 1, j), inside(i, j + 1), inside(i, j - 1)])
    border = {
        "E": lambda i: ("own", i, LAST),
        "W": lambda i: ("own", i, 0),
        "N": lambda j: ("own", LAST, j),
        "S": lambda j: ("own", 0, j),
    }
    beyond = {"E": ("EN", "ES"), "W": ("WN", "WS"), "N": ("NE", "NW"), "S": ("SE", "SW")}
    for side in "EWNS":
        high, low = beyond[side]
        for a in range(PASSES - 1):
            for i in range(SIDE):
                link(
                    (side, a, i),
                    [
                        border[side](i) if a == 0 else (side, a - 1, i),
                        (side, a + 1, i),
                        (side, a, i + 1) if i < LAST else (high, a, 0),
                        (side, a, i - 1) if i > 0 else (low, a, 0),
                    ],
                )
        for end, last in ((high, LAST), (low, 0)):
            link((end, 0, 0), [(side, 0, last), (end, 1, 0), (end, 0, 1), ("q", end)])
    powers = [lap[:CELLS]]
    for _ in range(PASSES - 1):
        powers.append(powers[-1] @ lap)
    return place, np.concatenate([p.T for p in powers], axis=1).astype(np.float32)


PLACE, WALKS = walk_operators()
WALKS_OWN = WALKS[:CELLS]


def pack_cells():
    west, east, far = [], [], []
    for a in range(PASSES):
        for i in range(SIDE):
            west.append((cell(i, a), cell(LAST - i, a), W_))
            east.append((cell(i, LAST - a), cell(LAST - i, LAST - a), E_))
    for a, b in CORNER:
        west.append((cell(b, a), cell(b, LAST - a), S_))
        east.append((cell(b, LAST - a), cell(b, a), S_))
    for a, b in CORNER:
        west.append((cell(LAST - b, a), cell(LAST - b, LAST - a), N_))
        east.append((cell(LAST - b, LAST - a), cell(LAST - b, a), N_))
    west += [(cell(LAST, 0), cell(LAST, LAST), N_), (cell(0, 0), cell(0, LAST), S_)]
    east += [(cell(LAST, LAST), cell(LAST, 0), N_), (cell(0, LAST), cell(0, 0), S_)]
    north_south = []
    for a in range(PASSES):
        for j in range(SIDE):
            north_south.append((cell(a, j), cell(a, LAST - j), S_))
    for a in range(PASSES):
        for j in range(SIDE):
            north_south.append((cell(LAST - a, j), cell(LAST - a, LAST - j), N_))
    own_q = [
        (cell(0, LAST), cell(LAST, LAST), E_),
        (cell(LAST, LAST), cell(0, LAST), E_),
        (cell(0, 0), cell(LAST, 0), W_),
        (cell(LAST, 0), cell(0, 0), W_),
    ]
    return west, east, north_south, own_q


def split(value):
    high = lax.reduce_precision(value, 8, 7)
    return high.astype(jnp.bfloat16), (value - high).astype(jnp.bfloat16)


def dot(left, right, dims):
    return lax.dot_general(left, right, (dims, ((), ())), preferred_element_type=jnp.float32)


def picked(table, flags, field):
    zero, one, edge = (np.array(column, np.int32)[:, None] for column in zip(*table))
    flag = jnp.zeros(zero.shape, jnp.int32)
    for k in range(4):
        flag = jnp.where(jnp.asarray(edge == k), flags[k], flag)
    index = jnp.where(flag == 1, jnp.asarray(one), jnp.asarray(zero))
    chosen = (lax.broadcasted_iota(jnp.int32, (len(table), CELLS), 1) == index).astype(jnp.bfloat16)
    high, low = split(field)
    return dot(chosen, high, ((1,), (1,))) + dot(chosen, low, ((1,), (1,)))


def halo_operator(flags, far_flags):
    by_flag = [np.zeros((NS_ROWS + 2 * EW_ROWS, PASSES * CELLS), np.float32) for _ in range(2)]
    edge = np.full((NS_ROWS + 2 * EW_ROWS, 1), -1, np.int32)

    def put(row, zero, one=None, which=-1):
        by_flag[0][row] = WALKS[PLACE[zero]]
        by_flag[1][row] = WALKS[PLACE[one or zero]]
        edge[row] = which

    for a in range(PASSES):
        for i in range(SIDE):
            k = a * SIDE + i
            put(k, ("N", a, i))
            put(48 + k, ("S", a, i))
            put(NS_ROWS + k, ("E", a, i))
            put(NS_ROWS + EW_ROWS + k, ("W", a, i))
    for k, (a, b) in enumerate(CORNER):
        put(96 + k, ("NE", a, b), ("NW", a, b), N_)
        put(99 + k, ("SE", a, b), ("SW", a, b), S_)
        put(102 + k, ("NW", a, b), ("NE", a, b), N_)
        put(105 + k, ("SW", a, b), ("SE", a, b), S_)
        put(108 + k, ("EN", a, b), ("ES", a, b), E_)
        put(111 + k, ("ES", a, b), ("EN", a, b), E_)
        put(114 + k, ("WN", a, b), ("WS", a, b), W_)
        put(117 + k, ("WS", a, b), ("WN", a, b), W_)
    put(120, ("q", "EN"), ("q", "ES"), E_)
    put(121, ("q", "ES"), ("q", "EN"), E_)
    put(122, ("q", "WN"), ("q", "WS"), W_)
    put(123, ("q", "WS"), ("q", "WN"), W_)
    flag = jnp.zeros(edge.shape, jnp.int32)
    for k in range(4):
        flag = jnp.where(jnp.asarray(edge == k), flags[k], flag)
    operator = jnp.where(
        flag == 1, jnp.asarray(by_flag[1], jnp.bfloat16), jnp.asarray(by_flag[0], jnp.bfloat16)
    )
    third = 2 * CELLS
    far_e, far_w = far_flags
    north_e = jnp.where(flags[N_] == 1, third + cell(LAST, 0), third + cell(LAST, LAST))
    north_w = jnp.where(flags[N_] == 1, third + cell(LAST, LAST), third + cell(LAST, 0))
    south_e = jnp.where(flags[S_] == 1, third + cell(0, 0), third + cell(0, LAST))
    south_w = jnp.where(flags[S_] == 1, third + cell(0, LAST), third + cell(0, 0))
    rows = lax.broadcasted_iota(jnp.int32, operator.shape, 0)
    columns = lax.broadcasted_iota(jnp.int32, operator.shape, 1)
    for row, column in (
        (NS_ROWS + 54, jnp.where(far_e == 1, south_e, north_e)),
        (NS_ROWS + 55, jnp.where(far_e == 1, north_e, south_e)),
        (NS_ROWS + EW_ROWS + 54, jnp.where(far_w == 1, south_w, north_w)),
        (NS_ROWS + EW_ROWS + 55, jnp.where(far_w == 1, north_w, south_w)),
    ):
        operator = jnp.where((rows == row) & (columns == column), jnp.bfloat16(1), operator)
    return operator


def local(control, perts, diffusivity, vertical, gain, edge_flip):
    member_count, level_count, cell_count = control.shape
    tile_count = lax.axis_size("tile")
    mem_count = lax.axis_size("mem")
    lanes = member_count * level_count
    flags = edge_flip[0]
    field = control.reshape(lanes, cell_count)
    west_table, east_table, ns_table, q_table = pack_cells()

    def shifted(value, by):
        return lax.ppermute(value, "tile", [(i, (i + by) % tile_count) for i in range(tile_count)])

    def swapped(value, mask):
        return lax.ppermute(value, "tile", [(i, i ^ mask) for i in range(tile_count)])

    squares = field * field
    high, low = split(squares)
    ones = jnp.ones((1, cell_count), jnp.bfloat16)
    norms = dot(ones, high, ((1,), (1,))) + dot(ones, low, ((1,), (1,)))
    flag_row = [jnp.broadcast_to(flags[k].astype(jnp.float32), (1, lanes)) for k in range(4)]
    tail = jnp.concatenate([flag_row[S_], flag_row[N_], norms, jnp.zeros((5, lanes), jnp.float32)])
    west_pack = jnp.concatenate([picked(west_table, flags, field), tail])
    east_pack = jnp.concatenate([picked(east_table, flags, field), tail])
    ends = jnp.array([0, LAST])
    pad = jnp.zeros((5, lanes), jnp.float32)
    west_far = jnp.concatenate([west_pack[0:1], west_pack[15:16], norms, pad])
    east_far = jnp.concatenate([east_pack[0:1], east_pack[15:16], norms, pad])
    from_east = shifted(west_pack, -1)
    from_west = shifted(east_pack, 1)
    from_east2 = shifted(west_far, -2)
    from_west2 = shifted(east_far, 2)

    own_q = picked(q_table, flags, field)
    strips = picked(ns_table, flags, field)
    window = from_west[58:59] + norms + from_east[58:59] + from_east2[2:3]
    by_row = [b * SIDE + a for a, b in CORNER]
    by_row += [b * SIDE + LAST - a for a, b in CORNER]
    corners_e = jnp.concatenate([from_east[k : k + 1] for k in by_row])
    corners_w = jnp.concatenate([from_west[k : k + 1] for k in by_row])
    q_rows = jnp.concatenate(
        [
            jnp.where(from_east[56:57] == 1, from_east2[0:1], own_q[0:1]),
            jnp.where(from_east[57:58] == 1, from_east2[1:2], own_q[1:2]),
            jnp.where(from_west[56:57] == 1, from_west2[0:1], own_q[2:3]),
            jnp.where(from_west[57:58] == 1, from_west2[1:2], own_q[3:4]),
        ]
    )
    ns_pack = jnp.concatenate(
        [strips, corners_e, corners_w, from_east[48:54], from_west[48:54], q_rows]
        + [flag_row[E_], flag_row[W_], window, jnp.zeros((1, lanes), jnp.float32)]
    )
    arrived = swapped(ns_pack, tile_count // 2)

    total = window + arrived[126:127]
    mask = 4
    while mask < tile_count // 2:
        total = total + swapped(total, mask)
        mask *= 2

    high, low = split(field)
    own = jnp.asarray(WALKS_OWN, jnp.bfloat16)
    walks = dot(high, own, ((1,), (0,))) + dot(low, own, ((1,), (0,)))
    halo = jnp.concatenate([arrived, from_east, from_west])
    far_flags = (arrived[124, 0].astype(jnp.int32), arrived[125, 0].astype(jnp.int32))
    operator = halo_operator(flags, far_flags)
    high, low = split(halo)
    walks = walks + dot(high, operator, ((0,), (0,))) + dot(low, operator, ((0,), (0,)))
    rates = jnp.tile(diffusivity, member_count)[:, None]
    diffused = field + rates * (
        3.0 * walks[:, :cell_count]
        + rates * (3.0 * walks[:, cell_count : 2 * cell_count] + rates * walks[:, 2 * cell_count :])
    )
    diffused = diffused.reshape(member_count, level_count, cell_count)
    mix = jnp.einsum("lm,kmc->klc", vertical, diffused, precision=lax.Precision.HIGHEST)
    term = jnp.sum(perts.astype(jnp.float32) * (gain[None] * mix), axis=0)
    pieces = term.reshape(mem_count, level_count // mem_count, cell_count)
    pieces = lax.all_to_all(pieces, "mem", 0, 0, tiled=True)
    members_all = member_count * mem_count
    increment = jnp.sum(pieces, axis=0) / jnp.sqrt(jnp.float32(members_all - 1))
    norm_count = level_count * cell_count * tile_count
    member_cost = 0.5 * jnp.sum(total.reshape(member_count, level_count), axis=1) / norm_count
    return (increment, member_cost)


def solution(mesh):
    placed = (
        P("mem", None, "tile"),
        P("mem", None, "tile"),
        P(),
        P(),
        P(None, "tile"),
        P("tile", None),
    )
    return jax.shard_map(
        local, mesh=mesh, in_specs=placed, out_specs=(P("mem", "tile"), P("mem")), check_vma=False
    )
```

```python
import jax
import jax.numpy as jnp
import numpy as np
from jax import lax
from jax.experimental import pallas as pl
from jax.experimental.pallas import tpu as pltpu
from jax.sharding import PartitionSpec as P

PASSES = 3
SIDE = 16
CELLS = SIDE * SIDE
CORNER = ((0, 0), (0, 1), (1, 0))
LAST = SIDE - 1

EW_ROWS = 64
NS_ROWS = 128
S_, E_, N_, W_ = range(4)


def cell(row, col):
    return row * SIDE + col


def walk_operators():
    names = [("own", i, j) for i in range(SIDE) for j in range(SIDE)]
    for side in "EWNS":
        names += [(side, a, i) for a in range(PASSES) for i in range(SIDE)]
    ends = ("EN", "ES", "WN", "WS", "NE", "NW", "SE", "SW")
    for end in ends:
        names += [(end, a, b) for a, b in CORNER]
    names += [("q", end) for end in ends]
    place = {name: k for k, name in enumerate(names)}
    size = len(names)
    lap = np.zeros((size, size), np.int64)

    def link(name, others):
        row = place[name]
        lap[row, row] -= 4
        for other in others:
            lap[row, place[other]] += 1

    def inside(i, j):
        if i < 0:
            return ("S", -1 - i, j)
        if i > LAST:
            return ("N", i - SIDE, j)
        if j < 0:
            return ("W", -1 - j, i)
        if j > LAST:
            return ("E", j - SIDE, i)
        return ("own", i, j)

    for i in range(SIDE):
        for j in range(SIDE):
            link(("own", i, j), [inside(i + 1, j), inside(i - 1, j), inside(i, j + 1), inside(i, j - 1)])
    border = {
        "E": lambda i: ("own", i, LAST),
        "W": lambda i: ("own", i, 0),
        "N": lambda j: ("own", LAST, j),
        "S": lambda j: ("own", 0, j),
    }
    beyond = {"E": ("EN", "ES"), "W": ("WN", "WS"), "N": ("NE", "NW"), "S": ("SE", "SW")}
    for side in "EWNS":
        high, low = beyond[side]
        for a in range(PASSES - 1):
            for i in range(SIDE):
                link(
                    (side, a, i),
                    [
                        border[side](i) if a == 0 else (side, a - 1, i),
                        (side, a + 1, i),
                        (side, a, i + 1) if i < LAST else (high, a, 0),
                        (side, a, i - 1) if i > 0 else (low, a, 0),
                    ],
                )
        for end, last in ((high, LAST), (low, 0)):
            link((end, 0, 0), [(side, 0, last), (end, 1, 0), (end, 0, 1), ("q", end)])
    powers = [lap[:CELLS]]
    for _ in range(PASSES - 1):
        powers.append(powers[-1] @ lap)
    return place, np.concatenate([p.T for p in powers], axis=1).astype(np.float32)


PLACE, WALKS = walk_operators()
WALKS_OWN = WALKS[:CELLS]


def pack_cells():
    west, east, far = [], [], []
    for a in range(PASSES):
        for i in range(SIDE):
            west.append((cell(i, a), cell(LAST - i, a), W_))
            east.append((cell(i, LAST - a), cell(LAST - i, LAST - a), E_))
    for a, b in CORNER:
        west.append((cell(b, a), cell(b, LAST - a), S_))
        east.append((cell(b, LAST - a), cell(b, a), S_))
    for a, b in CORNER:
        west.append((cell(LAST - b, a), cell(LAST - b, LAST - a), N_))
        east.append((cell(LAST - b, LAST - a), cell(LAST - b, a), N_))
    west += [(cell(LAST, 0), cell(LAST, LAST), N_), (cell(0, 0), cell(0, LAST), S_)]
    east += [(cell(LAST, LAST), cell(LAST, 0), N_), (cell(0, LAST), cell(0, 0), S_)]
    north_south = []
    for a in range(PASSES):
        for j in range(SIDE):
            north_south.append((cell(a, j), cell(a, LAST - j), S_))
    for a in range(PASSES):
        for j in range(SIDE):
            north_south.append((cell(LAST - a, j), cell(LAST - a, LAST - j), N_))
    own_q = [
        (cell(0, LAST), cell(LAST, LAST), E_),
        (cell(LAST, LAST), cell(0, LAST), E_),
        (cell(0, 0), cell(LAST, 0), W_),
        (cell(LAST, 0), cell(0, 0), W_),
    ]
    return west, east, north_south, own_q


def split(value):
    high = value.astype(jnp.bfloat16)
    return high, (value - high.astype(jnp.float32)).astype(jnp.bfloat16)


def dot(left, right, dims=((1,), (0,))):
    return lax.dot_general(left, right, (dims, ((), ())), preferred_element_type=jnp.float32)


def table_columns(table):
    rows = np.zeros((len(table), 8), np.int32)
    rows[:, :3] = np.array(table, np.int32)
    return rows


def per_row(edge, flags, shape):
    flag = jnp.zeros(shape, jnp.int32)
    for k in range(4):
        flag = jnp.where(edge == k, flags[k], flag)
    return flag


def pack_kernel(field_ref, flip_ref, table_ref, west_ref, east_ref, far_w_ref, far_e_ref, strips_ref):
    field = field_ref[...].reshape(-1, CELLS)
    lanes = field.shape[0]
    flags = [flip_ref[0, k] for k in range(4)]
    edge = table_ref[:, 2:3]
    flag = per_row(edge, flags, edge.shape)
    index = jnp.where(flag == 1, table_ref[:, 1:2], table_ref[:, 0:1])
    lane = lax.broadcasted_iota(jnp.int32, (edge.shape[0], CELLS), 1)
    chosen = jnp.where(lane == index, 1.0, 0.0).astype(jnp.bfloat16)
    high, low = split(field)
    nt = ((1,), (1,))
    rows = dot(chosen, high, nt) + dot(chosen, low, nt)
    high, low = split(field * field)
    ones = jnp.ones((8, CELLS), jnp.bfloat16)
    norms = (dot(ones, high, nt) + dot(ones, low, nt))[0:1]
    level = [jnp.full((1, lanes), flags[k].astype(jnp.float32)) for k in range(4)]
    for ref, far_ref, start in ((west_ref, far_w_ref, 0), (east_ref, far_e_ref, 56)):
        ref[0:56] = rows[start : start + 56]
        ref[56:57] = level[S_]
        ref[57:58] = level[N_]
        ref[58:59] = norms
        ref[59:64] = jnp.zeros((5, lanes), jnp.float32)
        far_ref[0:1] = rows[start : start + 1]
        far_ref[1:2] = rows[start + 15 : start + 16]
        far_ref[2:3] = norms
        far_ref[3:8] = jnp.zeros((5, lanes), jnp.float32)
    strips_ref[0:100] = rows[112:212]
    strips_ref[100:101] = level[E_]
    strips_ref[101:102] = level[W_]
    strips_ref[102:103] = norms
    strips_ref[103:104] = jnp.zeros((1, lanes), jnp.float32)


def relay_kernel(strips_ref, east_ref, west_ref, east2_ref, west2_ref, out_ref):
    out_ref[0:96] = strips_ref[0:96]
    row = 96
    for ref in (east_ref, west_ref):
        for a, b in CORNER:
            out_ref[row : row + 1] = ref[b * SIDE + a : b * SIDE + a + 1]
            row += 1
        for a, b in CORNER:
            out_ref[row : row + 1] = ref[b * SIDE + LAST - a : b * SIDE + SIDE - a]
            row += 1
    out_ref[108:114] = east_ref[48:54]
    out_ref[114:120] = west_ref[48:54]
    out_ref[120:122] = jnp.where(east_ref[56:58] == 1, east2_ref[0:2], strips_ref[96:98])
    out_ref[122:124] = jnp.where(west_ref[56:58] == 1, west2_ref[0:2], strips_ref[98:100])
    out_ref[124:126] = strips_ref[100:102]
    window = west_ref[58:59] + strips_ref[102:103] + east_ref[58:59] + east2_ref[2:3]
    out_ref[126:127] = window
    out_ref[127:128] = jnp.zeros_like(window)


def rate_column(diffusivity_ref, member_count):
    levels = diffusivity_ref.shape[1]
    here = lax.broadcasted_iota(jnp.int32, (levels, levels), 0)
    there = lax.broadcasted_iota(jnp.int32, (levels, levels), 1)
    column = jnp.sum(jnp.where(here == there, diffusivity_ref[...], 0.0), axis=1, keepdims=True)
    return jnp.concatenate([column] * member_count, axis=0)


def weighted(walks, rates):
    one, two, three = (walks[:, k * CELLS : (k + 1) * CELLS] for k in range(PASSES))
    return rates * (3.0 * one + rates * (3.0 * two + rates * three))


def own_kernel(
    field_ref, diffusivity_ref, vertical_ref, flip_ref, walks_ref, zero_ref, one_ref, edge_ref,
    base_ref, operator_ref, high_ref, low_ref,
):
    member_count, level_count, _ = field_ref.shape
    field = field_ref[...].reshape(-1, CELLS)
    rates = rate_column(diffusivity_ref, member_count)
    high, low = split(field)
    walks = dot(high, walks_ref[...]) + dot(low, walks_ref[...])
    base_ref[...] = field + weighted(walks, rates)
    flags = [flip_ref[0, k] for k in range(4)]
    flag = per_row(edge_ref[:, 0:1], flags, (edge_ref.shape[0], 1))
    flag = jnp.broadcast_to(flag, zero_ref.shape) == 1
    operator_ref[...] = jnp.where(
        flag, one_ref[...].astype(jnp.float32), zero_ref[...].astype(jnp.float32)
    ).astype(jnp.bfloat16)
    lanes = member_count * level_count
    across = jnp.concatenate([vertical_ref[...]] * member_count, axis=1)
    whole = jnp.concatenate([across] * member_count, axis=0)
    here = lax.broadcasted_iota(jnp.int32, (lanes, lanes), 0) // level_count
    there = lax.broadcasted_iota(jnp.int32, (lanes, lanes), 1) // level_count
    high, low = split(jnp.where(here == there, whole, 0.0))
    high_ref[...] = high
    low_ref[...] = low


def final_kernel(
    base_ref, operator_ref, high_ref, low_ref, arrived_ref, east_ref, west_ref, diffusivity_ref, flip_ref,
    perts_ref, gain_ref, term_ref,
):
    member_count, level_count, _ = perts_ref.shape
    rates = rate_column(diffusivity_ref, member_count)
    halo = jnp.concatenate([arrived_ref[...], east_ref[...], west_ref[...]], axis=0)
    flags = [flip_ref[0, k] for k in range(4)]
    north_e = jnp.where(flags[N_] == 1, cell(LAST, 0), cell(LAST, LAST))
    north_w = jnp.where(flags[N_] == 1, cell(LAST, LAST), cell(LAST, 0))
    south_e = jnp.where(flags[S_] == 1, cell(0, 0), cell(0, LAST))
    south_w = jnp.where(flags[S_] == 1, cell(0, LAST), cell(0, 0))
    far_e = arrived_ref[124:125, 0:1] == 1
    far_w = arrived_ref[125:126, 0:1] == 1
    rows = lax.broadcasted_iota(jnp.int32, (halo.shape[0], 1), 0)
    target = jnp.full(rows.shape, -1, jnp.int32)
    for row, yes, no, far in (
        (NS_ROWS + 54, south_e, north_e, far_e),
        (NS_ROWS + 55, north_e, south_e, far_e),
        (NS_ROWS + EW_ROWS + 54, south_w, north_w, far_w),
        (NS_ROWS + EW_ROWS + 55, north_w, south_w, far_w),
    ):
        target = jnp.where(rows == row, jnp.where(far, yes, no), target)
    lane = lax.broadcasted_iota(jnp.int32, (halo.shape[0], CELLS), 1)
    corner = jnp.where(lane == target, 1.0, 0.0).astype(jnp.bfloat16)
    high, low = split(halo.T)
    operator = operator_ref[...]
    walks = dot(high, operator) + dot(low, operator)
    extra = dot(high, corner) + dot(low, corner)
    diffused = base_ref[...] + weighted(walks, rates) + rates * rates * rates * extra
    high, low = split(diffused)
    mix = dot(high_ref[...], high) + dot(high_ref[...], low) + dot(low_ref[...], high)
    total = jnp.zeros((level_count, CELLS), jnp.float32)
    for k in range(member_count):
        rows = slice(k * level_count, (k + 1) * level_count)
        total = total + perts_ref[k].astype(jnp.float32) * mix[rows]
    term_ref[...] = (gain_ref[...] * total).reshape(term_ref.shape)


def halo_rows():
    by_flag = [np.zeros((NS_ROWS + 2 * EW_ROWS, PASSES * CELLS), np.float32) for _ in range(2)]
    edge = np.full((NS_ROWS + 2 * EW_ROWS, 8), -1, np.int32)

    def put(row, zero, one=None, which=-1):
        by_flag[0][row] = WALKS[PLACE[zero]]
        by_flag[1][row] = WALKS[PLACE[one or zero]]
        edge[row] = which

    for a in range(PASSES):
        for i in range(SIDE):
            k = a * SIDE + i
            put(k, ("N", a, i))
            put(48 + k, ("S", a, i))
            put(NS_ROWS + k, ("E", a, i))
            put(NS_ROWS + EW_ROWS + k, ("W", a, i))
    for k, (a, b) in enumerate(CORNER):
        put(96 + k, ("NE", a, b), ("NW", a, b), N_)
        put(99 + k, ("SE", a, b), ("SW", a, b), S_)
        put(102 + k, ("NW", a, b), ("NE", a, b), N_)
        put(105 + k, ("SW", a, b), ("SE", a, b), S_)
        put(108 + k, ("EN", a, b), ("ES", a, b), E_)
        put(111 + k, ("ES", a, b), ("EN", a, b), E_)
        put(114 + k, ("WN", a, b), ("WS", a, b), W_)
        put(117 + k, ("WS", a, b), ("WN", a, b), W_)
    put(120, ("q", "EN"), ("q", "ES"), E_)
    put(121, ("q", "ES"), ("q", "EN"), E_)
    put(122, ("q", "WN"), ("q", "WS"), W_)
    put(123, ("q", "WS"), ("q", "WN"), W_)
    return by_flag[0], by_flag[1], edge


def vmem(count):
    return [pl.BlockSpec(memory_space=pltpu.VMEM)] * count


SMEM = pl.BlockSpec(memory_space=pltpu.SMEM)


def local(control, perts, diffusivity, vertical, gain, edge_flip):
    member_count, level_count, cell_count = control.shape
    tile_count = lax.axis_size("tile")
    mem_count = lax.axis_size("mem")
    lanes = member_count * level_count
    west_table, east_table, ns_table, q_table = pack_cells()

    def shifted(value, by):
        return lax.ppermute(value, "tile", [(i, (i + by) % tile_count) for i in range(tile_count)])

    def swapped(value, mask):
        return lax.ppermute(value, "tile", [(i, i ^ mask) for i in range(tile_count)])

    def rows_of(count):
        return jax.ShapeDtypeStruct((count, lanes), jnp.float32)

    table = table_columns(west_table + east_table + ns_table + q_table + [(0, 0, -1)] * 4)
    west_pack, east_pack, west_far, east_far, strips = pl.pallas_call(
        pack_kernel,
        out_shape=[rows_of(EW_ROWS), rows_of(EW_ROWS), rows_of(8), rows_of(8), rows_of(104)],
        in_specs=vmem(1) + [SMEM] + vmem(1),
        out_specs=vmem(5),
        name="packs",
    )(control, edge_flip, jnp.asarray(table))
    from_east2 = shifted(west_far, -2)
    from_west2 = shifted(east_far, 2)
    from_east = shifted(west_pack, -1)
    from_west = shifted(east_pack, 1)

    ns_pack = pl.pallas_call(
        relay_kernel,
        out_shape=rows_of(NS_ROWS),
        in_specs=vmem(5),
        out_specs=vmem(1)[0],
        name="relay",
    )(strips, from_east, from_west, from_east2, from_west2)
    arrived = swapped(ns_pack, tile_count // 2)

    zero, one, edge = halo_rows()
    spread = diffusivity.reshape(1, level_count)
    wide = PASSES * cell_count
    base, operator, high, low = pl.pallas_call(
        own_kernel,
        out_shape=[
            jax.ShapeDtypeStruct((lanes, cell_count), jnp.float32),
            jax.ShapeDtypeStruct((NS_ROWS + 2 * EW_ROWS, wide), jnp.bfloat16),
            jax.ShapeDtypeStruct((lanes, lanes), jnp.bfloat16),
            jax.ShapeDtypeStruct((lanes, lanes), jnp.bfloat16),
        ],
        in_specs=vmem(3) + [SMEM] + vmem(4),
        out_specs=vmem(4),
        name="own_cells",
    )(
        control,
        spread,
        vertical,
        edge_flip,
        jnp.asarray(WALKS_OWN, jnp.bfloat16),
        jnp.asarray(zero, jnp.bfloat16),
        jnp.asarray(one, jnp.bfloat16),
        jnp.asarray(edge),
    )

    sums = jnp.broadcast_to(ns_pack[126:127] + arrived[126:127], (8, lanes))
    groups = [
        [low_bits + 32 * half + 4 * k for k in range(8)] for half in range(2) for low_bits in range(4)
    ]
    sums = lax.all_to_all(sums, "tile", 0, 0, tiled=True, axis_index_groups=groups)

    pieces = pl.pallas_call(
        final_kernel,
        out_shape=jax.ShapeDtypeStruct((mem_count, level_count // mem_count, cell_count), jnp.float32),
        in_specs=vmem(8) + [SMEM] + vmem(2),
        out_specs=vmem(1)[0],
        name="localized",
    )(base, operator, high, low, arrived, from_east, from_west, spread, edge_flip, perts, gain)
    pieces = lax.all_to_all(pieces, "mem", 0, 0, tiled=True)
    members_all = member_count * mem_count
    increment = jnp.sum(pieces, axis=0) / jnp.sqrt(jnp.float32(members_all - 1))
    norm_count = level_count * cell_count * tile_count
    member_cost = 0.5 * jnp.sum(sums.reshape(8, member_count, level_count), axis=(0, 2)) / norm_count
    return (increment, member_cost)


def solution(mesh):
    placed = (
        P("mem", None, "tile"),
        P("mem", None, "tile"),
        P(),
        P(),
        P(None, "tile"),
        P("tile", None),
    )
    return jax.shard_map(
        local, mesh=mesh, in_specs=placed, out_specs=(P("mem", "tile"), P("mem")), check_vma=False
    )
```

```python
import jax
import jax.numpy as jnp
import numpy as np
from jax import lax
from jax.experimental import pallas as pl
from jax.experimental.pallas import tpu as pltpu
from jax.sharding import PartitionSpec as P

PASSES = 3
SIDE = 16
CELLS = SIDE * SIDE
CORNER = ((0, 0), (0, 1), (1, 0))
LAST = SIDE - 1

EW_ROWS = 64
NS_ROWS = 128
GROUP = 16
S_, E_, N_, W_ = range(4)


def cell(row, col):
    return row * SIDE + col


def walk_operators():
    names = [("own", i, j) for i in range(SIDE) for j in range(SIDE)]
    for side in "EWNS":
        names += [(side, a, i) for a in range(PASSES) for i in range(SIDE)]
    ends = ("EN", "ES", "WN", "WS", "NE", "NW", "SE", "SW")
    for end in ends:
        names += [(end, a, b) for a, b in CORNER]
    names += [("q", end) for end in ends]
    place = {name: k for k, name in enumerate(names)}
    size = len(names)
    lap = np.zeros((size, size), np.int64)

    def link(name, others):
        row = place[name]
        lap[row, row] -= 4
        for other in others:
            lap[row, place[other]] += 1

    def inside(i, j):
        if i < 0:
            return ("S", -1 - i, j)
        if i > LAST:
            return ("N", i - SIDE, j)
        if j < 0:
            return ("W", -1 - j, i)
        if j > LAST:
            return ("E", j - SIDE, i)
        return ("own", i, j)

    for i in range(SIDE):
        for j in range(SIDE):
            link(("own", i, j), [inside(i + 1, j), inside(i - 1, j), inside(i, j + 1), inside(i, j - 1)])
    border = {
        "E": lambda i: ("own", i, LAST),
        "W": lambda i: ("own", i, 0),
        "N": lambda j: ("own", LAST, j),
        "S": lambda j: ("own", 0, j),
    }
    beyond = {"E": ("EN", "ES"), "W": ("WN", "WS"), "N": ("NE", "NW"), "S": ("SE", "SW")}
    for side in "EWNS":
        high, low = beyond[side]
        for a in range(PASSES - 1):
            for i in range(SIDE):
                link(
                    (side, a, i),
                    [
                        border[side](i) if a == 0 else (side, a - 1, i),
                        (side, a + 1, i),
                        (side, a, i + 1) if i < LAST else (high, a, 0),
                        (side, a, i - 1) if i > 0 else (low, a, 0),
                    ],
                )
        for end, last in ((high, LAST), (low, 0)):
            link((end, 0, 0), [(side, 0, last), (end, 1, 0), (end, 0, 1), ("q", end)])
    powers = [lap[:CELLS]]
    for _ in range(PASSES - 1):
        powers.append(powers[-1] @ lap)
    return place, np.concatenate([p.T for p in powers], axis=1).astype(np.float32)


PLACE, WALKS = walk_operators()
WALKS_OWN = WALKS[:CELLS]


def pack_cells():
    west, east, far = [], [], []
    for a in range(PASSES):
        for i in range(SIDE):
            west.append((cell(i, a), cell(LAST - i, a), W_))
            east.append((cell(i, LAST - a), cell(LAST - i, LAST - a), E_))
    for a, b in CORNER:
        west.append((cell(b, a), cell(b, LAST - a), S_))
        east.append((cell(b, LAST - a), cell(b, a), S_))
    for a, b in CORNER:
        west.append((cell(LAST - b, a), cell(LAST - b, LAST - a), N_))
        east.append((cell(LAST - b, LAST - a), cell(LAST - b, a), N_))
    west += [(cell(LAST, 0), cell(LAST, LAST), N_), (cell(0, 0), cell(0, LAST), S_)]
    east += [(cell(LAST, LAST), cell(LAST, 0), N_), (cell(0, LAST), cell(0, 0), S_)]
    north_south = []
    for a in range(PASSES):
        for j in range(SIDE):
            north_south.append((cell(a, j), cell(a, LAST - j), S_))
    for a in range(PASSES):
        for j in range(SIDE):
            north_south.append((cell(LAST - a, j), cell(LAST - a, LAST - j), N_))
    own_q = [
        (cell(0, LAST), cell(LAST, LAST), E_),
        (cell(LAST, LAST), cell(0, LAST), E_),
        (cell(0, 0), cell(LAST, 0), W_),
        (cell(LAST, 0), cell(0, 0), W_),
    ]
    return west, east, north_south, own_q


def split(value):
    high = value.astype(jnp.bfloat16)
    return high, (value - high.astype(jnp.float32)).astype(jnp.bfloat16)


def dot(left, right, dims=((1,), (0,))):
    return lax.dot_general(left, right, (dims, ((), ())), preferred_element_type=jnp.float32)


def table_columns(table):
    rows = np.zeros((len(table), 8), np.int32)
    rows[:, :3] = np.array(table, np.int32)
    return rows


def per_row(edge, flags, shape):
    flag = jnp.zeros(shape, jnp.int32)
    for k in range(4):
        flag = jnp.where(edge == k, flags[k], flag)
    return flag


def pack_kernel(field_ref, flip_ref, place_ref, table_ref, first_ref, second_ref, far_ref, strips_ref):
    field = field_ref[...].reshape(-1, CELLS)
    lanes = field.shape[0]
    flags = [flip_ref[0, k] for k in range(4)]
    edge = table_ref[:, 2:3]
    flag = per_row(edge, flags, edge.shape)
    index = jnp.where(flag == 1, table_ref[:, 1:2], table_ref[:, 0:1])
    lane = lax.broadcasted_iota(jnp.int32, (edge.shape[0], CELLS), 1)
    chosen = jnp.where(lane == index, 1.0, 0.0).astype(jnp.bfloat16)
    high, low = split(field)
    nt = ((1,), (1,))
    rows = dot(chosen, high, nt) + dot(chosen, low, nt)
    high, low = split(field * field)
    ones = jnp.ones((8, CELLS), jnp.bfloat16)
    norms = (dot(ones, high, nt) + dot(ones, low, nt))[0:1]
    level = [jnp.full((1, lanes), flags[k].astype(jnp.float32)) for k in range(4)]
    west, east = rows[0:56], rows[56:112]
    even = place_ref[0, 0] % 2 == 0
    first_ref[0:56] = jnp.where(even, east, west)
    second_ref[0:56] = jnp.where(even, west, east)
    for ref in (first_ref, second_ref):
        ref[56:57] = level[S_]
        ref[57:58] = level[N_]
        ref[58:59] = norms
        ref[59:64] = jnp.zeros((5, lanes), jnp.float32)
    far_ref[0:1] = first_ref[0:1]
    far_ref[1:2] = first_ref[LAST : LAST + 1]
    far_ref[2:8] = jnp.zeros((6, lanes), jnp.float32)
    strips_ref[0:100] = rows[112:212]
    strips_ref[100:101] = level[E_]
    strips_ref[101:102] = level[W_]
    strips_ref[102:103] = norms
    strips_ref[103:104] = jnp.zeros((1, lanes), jnp.float32)


def second_kernel(second_ref, near_ref, out_ref):
    out_ref[0:59] = second_ref[0:59]
    out_ref[59:60] = near_ref[0:1]
    out_ref[60:61] = near_ref[LAST : LAST + 1]
    out_ref[61:62] = second_ref[58:59] + near_ref[58:59]
    out_ref[62:64] = jnp.zeros((2, out_ref.shape[1]), jnp.float32)


def third_kernel(second_ref, other_ref, wrap_ref, out_ref):
    out_ref[0:1] = other_ref[0:1] + wrap_ref[0:1]
    out_ref[1:2] = other_ref[LAST : LAST + 1] + wrap_ref[LAST : LAST + 1]
    out_ref[2:3] = second_ref[61:62] + other_ref[61:62]
    out_ref[3:8] = jnp.zeros((5, out_ref.shape[1]), jnp.float32)


def relay_kernel(strips_ref, second_ref, near_ref, other_ref, wrap_ref, back_ref, place_ref, out_ref):
    place = place_ref[0, 0]
    even = place % 2 == 0
    near = near_ref[...]
    other = other_ref[...] + wrap_ref[...]
    out_ref[0:96] = strips_ref[0:96]
    row = 96
    for pack, far in (
        (jnp.where(even, near, other), jnp.where(even, back_ref[0:2], other[59:61])),
        (jnp.where(even, other, near), jnp.where(even, other[59:61], back_ref[0:2])),
    ):
        side = (row - 96) // 6
        for a, b in CORNER:
            out_ref[row : row + 1] = pack[b * SIDE + a : b * SIDE + a + 1]
            out_ref[row + 3 : row + 4] = pack[b * SIDE + LAST - a : b * SIDE + SIDE - a]
            row += 1
        row += 3
        out_ref[108 + 6 * side : 114 + 6 * side] = pack[48:54]
        own = strips_ref[96 + 2 * side : 98 + 2 * side]
        out_ref[120 + 2 * side : 122 + 2 * side] = jnp.where(pack[56:58] == 1, far, own)
    out_ref[124:126] = strips_ref[100:102]
    y = place % 4
    out_ref[126:127] = jnp.where((y == 1) | (y == 2), second_ref[61:62] + other[61:62], back_ref[2:3])
    out_ref[127:128] = jnp.zeros((1, out_ref.shape[1]), jnp.float32)


def rate_column(diffusivity_ref, member_count):
    levels = diffusivity_ref.shape[1]
    here = lax.broadcasted_iota(jnp.int32, (levels, levels), 0)
    there = lax.broadcasted_iota(jnp.int32, (levels, levels), 1)
    column = jnp.sum(jnp.where(here == there, diffusivity_ref[...], 0.0), axis=1, keepdims=True)
    return jnp.concatenate([column] * member_count, axis=0)


def weighted(walks, rates):
    one, two, three = (walks[:, k * CELLS : (k + 1) * CELLS] for k in range(PASSES))
    return rates * (3.0 * one + rates * (3.0 * two + rates * three))


def own_kernel(
    field_ref, diffusivity_ref, vertical_ref, flip_ref, walks_ref, zero_ref, one_ref, edge_ref,
    base_ref, operator_ref, high_ref, low_ref,
):
    member_count, level_count, _ = field_ref.shape
    field = field_ref[...].reshape(-1, CELLS)
    rates = rate_column(diffusivity_ref, member_count)
    high, low = split(field)
    walks = dot(high, walks_ref[...]) + dot(low, walks_ref[...])
    base_ref[...] = field + weighted(walks, rates)
    flags = [flip_ref[0, k] for k in range(4)]
    flag = per_row(edge_ref[:, 0:1], flags, (edge_ref.shape[0], 1))
    flag = jnp.broadcast_to(flag, zero_ref.shape) == 1
    operator_ref[...] = jnp.where(
        flag, one_ref[...].astype(jnp.float32), zero_ref[...].astype(jnp.float32)
    ).astype(jnp.bfloat16)
    lanes = member_count * level_count
    across = jnp.concatenate([vertical_ref[...]] * member_count, axis=1)
    whole = jnp.concatenate([across] * member_count, axis=0)
    here = lax.broadcasted_iota(jnp.int32, (lanes, lanes), 0) // level_count
    there = lax.broadcasted_iota(jnp.int32, (lanes, lanes), 1) // level_count
    high, low = split(jnp.where(here == there, whole, 0.0))
    high_ref[...] = high
    low_ref[...] = low

def sums_kernel(sent_ref, arrived_ref, out_ref):
    out_ref[...] = jnp.broadcast_to(sent_ref[126:127] + arrived_ref[126:127], out_ref.shape)


def final_kernel(
    base_ref, operator_ref, high_ref, low_ref, arrived_ref, near_ref, other_ref, wrap_ref, far_ref, far2_ref,
    diffusivity_ref, flip_ref, place_ref, perts_ref, gain_ref, term_ref,
    halo_ref,
):
    member_count, level_count, _ = perts_ref.shape
    rates = rate_column(diffusivity_ref, member_count)
    place = place_ref[0, 0]
    even = place % 2 == 0
    near = near_ref[...]
    other = other_ref[...] + wrap_ref[...]
    halo_ref[0:NS_ROWS] = arrived_ref[...]
    halo_ref[NS_ROWS : NS_ROWS + EW_ROWS] = jnp.where(even, near, other)
    halo_ref[NS_ROWS + EW_ROWS :] = jnp.where(even, other, near)
    for here, start, row in ((GROUP - 1, NS_ROWS, 120), (0, NS_ROWS + EW_ROWS, 122)):
        for k, flag in ((0, 57), (1, 56)):
            flagged = (halo_ref[start + flag : start + flag + 1] == 1) & (place == here)
            old = halo_ref[row + k : row + k + 1]
            straight = far_ref[k : k + 1] + far2_ref[k : k + 1]
            halo_ref[row + k : row + k + 1] = jnp.where(flagged, straight, old)
    halo = halo_ref[...]
    flags = [flip_ref[0, k] for k in range(4)]
    north_e = jnp.where(flags[N_] == 1, cell(LAST, 0), cell(LAST, LAST))
    north_w = jnp.where(flags[N_] == 1, cell(LAST, LAST), cell(LAST, 0))
    south_e = jnp.where(flags[S_] == 1, cell(0, 0), cell(0, LAST))
    south_w = jnp.where(flags[S_] == 1, cell(0, LAST), cell(0, 0))
    far_e = arrived_ref[124:125, 0:1] == 1
    far_w = arrived_ref[125:126, 0:1] == 1
    rows = lax.broadcasted_iota(jnp.int32, (halo.shape[0], 1), 0)
    target = jnp.full(rows.shape, -1, jnp.int32)
    for row, yes, no, far in (
        (NS_ROWS + 54, south_e, north_e, far_e),
        (NS_ROWS + 55, north_e, south_e, far_e),
        (NS_ROWS + EW_ROWS + 54, south_w, north_w, far_w),
        (NS_ROWS + EW_ROWS + 55, north_w, south_w, far_w),
    ):
        target = jnp.where(rows == row, jnp.where(far, yes, no), target)
    lane = lax.broadcasted_iota(jnp.int32, (halo.shape[0], CELLS), 1)
    corner = jnp.where(lane == target, 1.0, 0.0).astype(jnp.bfloat16)
    high, low = split(halo.T)
    operator = operator_ref[...]
    walks = dot(high, operator) + dot(low, operator)
    extra = dot(high, corner) + dot(low, corner)
    diffused = base_ref[...] + weighted(walks, rates) + rates * rates * rates * extra
    high, low = split(diffused)
    mix = dot(high_ref[...], high) + dot(high_ref[...], low) + dot(low_ref[...], high)
    total = jnp.zeros((level_count, CELLS), jnp.float32)
    for k in range(member_count):
        rows = slice(k * level_count, (k + 1) * level_count)
        total = total + perts_ref[k].astype(jnp.float32) * mix[rows]
    term_ref[...] = (gain_ref[...] * total).reshape(term_ref.shape)


def halo_rows():
    by_flag = [np.zeros((NS_ROWS + 2 * EW_ROWS, PASSES * CELLS), np.float32) for _ in range(2)]
    edge = np.full((NS_ROWS + 2 * EW_ROWS, 8), -1, np.int32)

    def put(row, zero, one=None, which=-1):
        by_flag[0][row] = WALKS[PLACE[zero]]
        by_flag[1][row] = WALKS[PLACE[one or zero]]
        edge[row] = which

    for a in range(PASSES):
        for i in range(SIDE):
            k = a * SIDE + i
            put(k, ("N", a, i))
            put(48 + k, ("S", a, i))
            put(NS_ROWS + k, ("E", a, i))
            put(NS_ROWS + EW_ROWS + k, ("W", a, i))
    for k, (a, b) in enumerate(CORNER):
        put(96 + k, ("NE", a, b), ("NW", a, b), N_)
        put(99 + k, ("SE", a, b), ("SW", a, b), S_)
        put(102 + k, ("NW", a, b), ("NE", a, b), N_)
        put(105 + k, ("SW", a, b), ("SE", a, b), S_)
        put(108 + k, ("EN", a, b), ("ES", a, b), E_)
        put(111 + k, ("ES", a, b), ("EN", a, b), E_)
        put(114 + k, ("WN", a, b), ("WS", a, b), W_)
        put(117 + k, ("WS", a, b), ("WN", a, b), W_)
    put(120, ("q", "EN"), ("q", "ES"), E_)
    put(121, ("q", "ES"), ("q", "EN"), E_)
    put(122, ("q", "WN"), ("q", "WS"), W_)
    put(123, ("q", "WS"), ("q", "WN"), W_)
    return by_flag[0], by_flag[1], edge


def vmem(count):
    return [pl.BlockSpec(memory_space=pltpu.VMEM)] * count


SMEM = pl.BlockSpec(memory_space=pltpu.SMEM)


def room(mebibytes):
    return pltpu.CompilerParams(vmem_limit_bytes=mebibytes * 2**20)


def local(control, perts, diffusivity, vertical, gain, edge_flip):
    member_count, level_count, cell_count = control.shape
    tile_count = lax.axis_size("tile")
    mem_count = lax.axis_size("mem")
    lanes = member_count * level_count
    west_table, east_table, ns_table, q_table = pack_cells()

    place = (lax.axis_index("tile") % GROUP).astype(jnp.int32).reshape(1, 1)

    def exchanged(value, pairs):
        both = [(i % tile_count, j % tile_count) for i, j in pairs]
        return lax.ppermute(value, "tile", both + [(j, i) for i, j in both])

    def swapped(value, mask):
        return lax.ppermute(value, "tile", [(i, i ^ mask) for i in range(tile_count)])

    half = tile_count // 2
    edges = range(GROUP, tile_count + 1, GROUP)
    pairs = [(i, i + 1) for i in range(0, tile_count, 2)]
    between = [(i, i + 1) for i in range(1, tile_count, 2) if (i + 1) % GROUP]

    def rows_of(count):
        return jax.ShapeDtypeStruct((count, lanes), jnp.float32)

    table = table_columns(west_table + east_table + ns_table + q_table + [(0, 0, -1)] * 4)
    first, second, far, strips = pl.pallas_call(
        pack_kernel,
        out_shape=[rows_of(count) for count in (EW_ROWS, EW_ROWS, 8, 104)],
        in_specs=vmem(1) + [SMEM, SMEM] + vmem(1),
        out_specs=vmem(4),
        name="packs",
    )(control, edge_flip, place, jnp.asarray(table))
    direct = [((k + half + 1) % tile_count, k - 1) for k in edges]
    direct += [((k + half - 2) % tile_count, k % tile_count) for k in edges]
    wrap = exchanged(second, [(k - 1, k) for k in edges])
    far1 = lax.ppermute(far, "tile", [pair for pair in direct if pair[1] < half])
    near = exchanged(first, pairs)
    control_there, first = lax.optimization_barrier((control, first))
    zero, one, edge = halo_rows()
    spread = diffusivity.reshape(1, level_count)
    wide = PASSES * cell_count
    base, operator, high, low = pl.pallas_call(
        own_kernel,
        out_shape=[
            jax.ShapeDtypeStruct((lanes, cell_count), jnp.float32),
            jax.ShapeDtypeStruct((NS_ROWS + 2 * EW_ROWS, wide), jnp.bfloat16),
            jax.ShapeDtypeStruct((lanes, lanes), jnp.bfloat16),
            jax.ShapeDtypeStruct((lanes, lanes), jnp.bfloat16),
        ],
        in_specs=vmem(3) + [SMEM] + vmem(4),
        out_specs=vmem(4),
        name="own_cells",
    )(
        control_there,
        spread,
        vertical,
        edge_flip,
        jnp.asarray(WALKS_OWN, jnp.bfloat16),
        jnp.asarray(zero, jnp.bfloat16),
        jnp.asarray(one, jnp.bfloat16),
        jnp.asarray(edge),
    )
    near, base = lax.optimization_barrier((near, base))
    second = pl.pallas_call(
        second_kernel, out_shape=rows_of(EW_ROWS), in_specs=vmem(2), out_specs=vmem(1)[0], name="second", compiler_params=room(4)
    )(second, near)
    other = exchanged(second, between)
    back = pl.pallas_call(
        third_kernel, out_shape=rows_of(8), in_specs=vmem(3), out_specs=vmem(1)[0], name="third", compiler_params=room(4)
    )(second, other, wrap)
    back = exchanged(back, pairs)
    ns_pack = pl.pallas_call(
        relay_kernel,
        out_shape=rows_of(NS_ROWS),
        in_specs=vmem(6) + [SMEM],
        out_specs=vmem(1)[0],
        name="relay", compiler_params=room(4),
    )(strips, second, near, other, wrap, back, place)
    arrived = exchanged(ns_pack, [(i, i + half) for i in range(half)])
    far, ns_pack, far1 = lax.optimization_barrier((far, ns_pack, far1))
    far2 = lax.ppermute(far, "tile", [pair for pair in direct if pair[1] >= half])

    arrived, far2 = lax.optimization_barrier((arrived, far2))
    sums = pl.pallas_call(
        sums_kernel,
        out_shape=rows_of(64),
        in_specs=vmem(2),
        out_specs=vmem(1)[0],
        name="sums",
        compiler_params=room(4),
    )(ns_pack, arrived)
    groups = [
        [low_bits + half * k + 4 * i for i in range(8)] for k in range(2) for low_bits in range(4)
    ]
    sums = lax.all_to_all(sums, "tile", 0, 0, tiled=True, axis_index_groups=groups)
    pieces = pl.pallas_call(
        final_kernel,
        out_shape=jax.ShapeDtypeStruct((mem_count, level_count // mem_count, cell_count), jnp.float32),
        in_specs=vmem(11) + [SMEM, SMEM] + vmem(2),
        out_specs=vmem(1)[0],
        scratch_shapes=[pltpu.VMEM((NS_ROWS + 2 * EW_ROWS, lanes), jnp.float32)],
        name="localized",
        compiler_params=room(16),
    )(
        base, operator, high, low, arrived, near, other, wrap, far1, far2,
        spread, edge_flip, place, perts, gain,
    )
    pieces, sums = lax.optimization_barrier((pieces, sums))
    pieces = lax.all_to_all(pieces, "mem", 0, 0, tiled=True)
    members_all = member_count * mem_count
    increment = jnp.sum(pieces, axis=0) / jnp.sqrt(jnp.float32(members_all - 1))
    norm_count = level_count * cell_count * tile_count
    sums = jnp.sum(sums.reshape(64, member_count, level_count), axis=(0, 2)) / 8.0
    member_cost = 0.5 * sums / norm_count
    return (increment, member_cost)


def solution(mesh):
    placed = (
        P("mem", None, "tile"),
        P("mem", None, "tile"),
        P(),
        P(),
        P(None, "tile"),
        P("tile", None),
    )
    return jax.shard_map(
        local, mesh=mesh, in_specs=placed, out_specs=(P("mem", "tile"), P("mem")), check_vma=False
    )
```

```python
import jax
import jax.numpy as jnp
import numpy as np
from jax import lax
from jax.experimental import pallas as pl
from jax.experimental.pallas import tpu as pltpu
from jax.sharding import PartitionSpec as P

PASSES = 3
SIDE = 16
CELLS = SIDE * SIDE
CORNER = ((0, 0), (0, 1), (1, 0))
LAST = SIDE - 1

EW_ROWS = 64
NS_ROWS = 128
GROUP = 16
S_, E_, N_, W_ = range(4)


def cell(row, col):
    return row * SIDE + col


def walk_operators():
    names = [("own", i, j) for i in range(SIDE) for j in range(SIDE)]
    for side in "EWNS":
        names += [(side, a, i) for a in range(PASSES) for i in range(SIDE)]
    ends = ("EN", "ES", "WN", "WS", "NE", "NW", "SE", "SW")
    for end in ends:
        names += [(end, a, b) for a, b in CORNER]
    names += [("q", end) for end in ends]
    place = {name: k for k, name in enumerate(names)}
    size = len(names)
    lap = np.zeros((size, size), np.int64)

    def link(name, others):
        row = place[name]
        lap[row, row] -= 4
        for other in others:
            lap[row, place[other]] += 1

    def inside(i, j):
        if i < 0:
            return ("S", -1 - i, j)
        if i > LAST:
            return ("N", i - SIDE, j)
        if j < 0:
            return ("W", -1 - j, i)
        if j > LAST:
            return ("E", j - SIDE, i)
        return ("own", i, j)

    for i in range(SIDE):
        for j in range(SIDE):
            link(("own", i, j), [inside(i + 1, j), inside(i - 1, j), inside(i, j + 1), inside(i, j - 1)])
    border = {
        "E": lambda i: ("own", i, LAST),
        "W": lambda i: ("own", i, 0),
        "N": lambda j: ("own", LAST, j),
        "S": lambda j: ("own", 0, j),
    }
    beyond = {"E": ("EN", "ES"), "W": ("WN", "WS"), "N": ("NE", "NW"), "S": ("SE", "SW")}
    for side in "EWNS":
        high, low = beyond[side]
        for a in range(PASSES - 1):
            for i in range(SIDE):
                link(
                    (side, a, i),
                    [
                        border[side](i) if a == 0 else (side, a - 1, i),
                        (side, a + 1, i),
                        (side, a, i + 1) if i < LAST else (high, a, 0),
                        (side, a, i - 1) if i > 0 else (low, a, 0),
                    ],
                )
        for end, last in ((high, LAST), (low, 0)):
            link((end, 0, 0), [(side, 0, last), (end, 1, 0), (end, 0, 1), ("q", end)])
    powers = [lap[:CELLS]]
    for _ in range(PASSES - 1):
        powers.append(powers[-1] @ lap)
    return place, np.concatenate([p.T for p in powers], axis=1).astype(np.float32)


PLACE, WALKS = walk_operators()
WALKS_OWN = WALKS[:CELLS]


def pack_cells():
    west, east, far = [], [], []
    for a in range(PASSES):
        for i in range(SIDE):
            west.append((cell(i, a), cell(LAST - i, a), W_))
            east.append((cell(i, LAST - a), cell(LAST - i, LAST - a), E_))
    for a, b in CORNER:
        west.append((cell(b, a), cell(b, LAST - a), S_))
        east.append((cell(b, LAST - a), cell(b, a), S_))
    for a, b in CORNER:
        west.append((cell(LAST - b, a), cell(LAST - b, LAST - a), N_))
        east.append((cell(LAST - b, LAST - a), cell(LAST - b, a), N_))
    west += [(cell(LAST, 0), cell(LAST, LAST), N_), (cell(0, 0), cell(0, LAST), S_)]
    east += [(cell(LAST, LAST), cell(LAST, 0), N_), (cell(0, LAST), cell(0, 0), S_)]
    north_south = []
    for a in range(PASSES):
        for j in range(SIDE):
            north_south.append((cell(a, j), cell(a, LAST - j), S_))
    for a in range(PASSES):
        for j in range(SIDE):
            north_south.append((cell(LAST - a, j), cell(LAST - a, LAST - j), N_))
    own_q = [
        (cell(0, LAST), cell(LAST, LAST), E_),
        (cell(LAST, LAST), cell(0, LAST), E_),
        (cell(0, 0), cell(LAST, 0), W_),
        (cell(LAST, 0), cell(0, 0), W_),
    ]
    return west, east, north_south, own_q


def split(value):
    high = value.astype(jnp.bfloat16)
    return high, (value - high.astype(jnp.float32)).astype(jnp.bfloat16)


def dot(left, right, dims=((1,), (0,))):
    return lax.dot_general(left, right, (dims, ((), ())), preferred_element_type=jnp.float32)


def table_columns(table):
    rows = np.zeros((len(table), 8), np.int32)
    rows[:, :3] = np.array(table, np.int32)
    return rows


def per_row(edge, flags, shape):
    flag = jnp.zeros(shape, jnp.int32)
    for k in range(4):
        flag = jnp.where(edge == k, flags[k], flag)
    return flag


def pack_kernel(field_ref, flip_ref, place_ref, table_ref, first_ref, second_ref, wrap_ref, strips_ref):
    field = field_ref[...].reshape(-1, CELLS)
    lanes = field.shape[0]
    flags = [flip_ref[0, k] for k in range(4)]
    edge = table_ref[:, 2:3]
    flag = per_row(edge, flags, edge.shape)
    index = jnp.where(flag == 1, table_ref[:, 1:2], table_ref[:, 0:1])
    lane = lax.broadcasted_iota(jnp.int32, (edge.shape[0], CELLS), 1)
    chosen = jnp.where(lane == index, 1.0, 0.0).astype(jnp.bfloat16)
    high, low = split(field)
    nt = ((1,), (1,))
    rows = dot(chosen, high, nt) + dot(chosen, low, nt)
    high, low = split(field * field)
    ones = jnp.ones((8, CELLS), jnp.bfloat16)
    norms = (dot(ones, high, nt) + dot(ones, low, nt))[0:1]
    level = [jnp.full((1, lanes), flags[k].astype(jnp.float32)) for k in range(4)]
    west, east = rows[0:56], rows[56:112]
    even = place_ref[0, 0] % 2 == 0
    first_ref[0:56] = jnp.where(even, east, west)
    second_ref[0:56] = jnp.where(even, west, east)
    for ref in (first_ref, second_ref):
        ref[56:57] = level[S_]
        ref[57:58] = level[N_]
        ref[58:59] = norms
        ref[59:64] = jnp.zeros((5, lanes), jnp.float32)
    at_end = (place_ref[0, 0] == 0) | (place_ref[0, 0] == GROUP - 1)
    wrap_ref[...] = jnp.where(at_end, second_ref[...], first_ref[...])
    strips_ref[0:100] = rows[112:212]
    strips_ref[100:101] = level[E_]
    strips_ref[101:102] = level[W_]
    strips_ref[102:103] = norms
    strips_ref[103:104] = jnp.zeros((1, lanes), jnp.float32)


def second_kernel(second_ref, near_ref, out_ref):
    out_ref[0:59] = second_ref[0:59]
    out_ref[59:60] = near_ref[0:1]
    out_ref[60:61] = near_ref[LAST : LAST + 1]
    out_ref[61:62] = second_ref[58:59] + near_ref[58:59]
    out_ref[62:64] = jnp.zeros((2, out_ref.shape[1]), jnp.float32)


def across(place, other, wrap):
    return jnp.where((place == 0) | (place == GROUP - 1), wrap, other)


def third_kernel(second_ref, other_ref, wrap_ref, place_ref, out_ref):
    place = place_ref[0, 0]
    out_ref[0:1] = across(place, other_ref[0:1], wrap_ref[0:1])
    out_ref[1:2] = across(place, other_ref[LAST : LAST + 1], wrap_ref[LAST : LAST + 1])
    out_ref[2:3] = second_ref[61:62] + other_ref[61:62]
    out_ref[3:4] = wrap_ref[0:1]
    out_ref[4:5] = wrap_ref[LAST : LAST + 1]
    out_ref[5:8] = jnp.zeros((3, out_ref.shape[1]), jnp.float32)


def relay_kernel(strips_ref, second_ref, near_ref, other_ref, wrap_ref, back_ref, place_ref, out_ref, sums_ref):
    place = place_ref[0, 0]
    even = place % 2 == 0
    near = near_ref[...]
    other = across(place, other_ref[...], wrap_ref[...])
    out_ref[0:96] = strips_ref[0:96]
    row = 96
    for pack, far in (
        (jnp.where(even, near, other), jnp.where(even, back_ref[0:2], other[59:61])),
        (jnp.where(even, other, near), jnp.where(even, other[59:61], back_ref[0:2])),
    ):
        side = (row - 96) // 6
        for a, b in CORNER:
            out_ref[row : row + 1] = pack[b * SIDE + a : b * SIDE + a + 1]
            out_ref[row + 3 : row + 4] = pack[b * SIDE + LAST - a : b * SIDE + SIDE - a]
            row += 1
        row += 3
        out_ref[108 + 6 * side : 114 + 6 * side] = pack[48:54]
        own = strips_ref[96 + 2 * side : 98 + 2 * side]
        out_ref[120 + 2 * side : 122 + 2 * side] = jnp.where(pack[56:58] == 1, far, own)
    out_ref[124:126] = strips_ref[100:102]
    y = place % 4
    sums = jnp.where((y == 1) | (y == 2), second_ref[61:62] + other[61:62], back_ref[2:3])
    out_ref[126:128] = jnp.zeros((2, out_ref.shape[1]), jnp.float32)
    sums_ref[...] = jnp.broadcast_to(sums, sums_ref.shape)


def rate_column(diffusivity_ref, member_count):
    levels = diffusivity_ref.shape[1]
    here = lax.broadcasted_iota(jnp.int32, (levels, levels), 0)
    there = lax.broadcasted_iota(jnp.int32, (levels, levels), 1)
    column = jnp.sum(jnp.where(here == there, diffusivity_ref[...], 0.0), axis=1, keepdims=True)
    return jnp.concatenate([column] * member_count, axis=0)


def weighted(walks, rates):
    one, two, three = (walks[:, k * CELLS : (k + 1) * CELLS] for k in range(PASSES))
    return rates * (3.0 * one + rates * (3.0 * two + rates * three))


def own_kernel(
    field_ref, diffusivity_ref, vertical_ref, flip_ref, walks_ref, zero_ref, one_ref, edge_ref,
    base_ref, operator_ref, high_ref, low_ref,
):
    member_count, level_count, _ = field_ref.shape
    field = field_ref[...].reshape(-1, CELLS)
    rates = rate_column(diffusivity_ref, member_count)
    high, low = split(field)
    walks = dot(high, walks_ref[...]) + dot(low, walks_ref[...])
    base_ref[...] = field + weighted(walks, rates)
    flags = [flip_ref[0, k] for k in range(4)]
    flag = per_row(edge_ref[:, 0:1], flags, (edge_ref.shape[0], 1))
    flag = jnp.broadcast_to(flag, zero_ref.shape) == 1
    operator_ref[...] = jnp.where(
        flag, one_ref[...].astype(jnp.float32), zero_ref[...].astype(jnp.float32)
    ).astype(jnp.bfloat16)
    lanes = member_count * level_count
    across = jnp.concatenate([vertical_ref[...]] * member_count, axis=1)
    whole = jnp.concatenate([across] * member_count, axis=0)
    here = lax.broadcasted_iota(jnp.int32, (lanes, lanes), 0) // level_count
    there = lax.broadcasted_iota(jnp.int32, (lanes, lanes), 1) // level_count
    high, low = split(jnp.where(here == there, whole, 0.0))
    high_ref[...] = high
    low_ref[...] = low

def final_kernel(
    base_ref, operator_ref, high_ref, low_ref, arrived_ref, near_ref, other_ref, wrap_ref, back_ref,
    diffusivity_ref, flip_ref, place_ref, perts_ref, gain_ref, term_ref,
    halo_ref,
):
    member_count, level_count, _ = perts_ref.shape
    rates = rate_column(diffusivity_ref, member_count)
    place = place_ref[0, 0]
    even = place % 2 == 0
    near = near_ref[...]
    other = across(place, other_ref[...], wrap_ref[...])
    halo_ref[0:NS_ROWS] = arrived_ref[...]
    halo_ref[NS_ROWS : NS_ROWS + EW_ROWS] = jnp.where(even, near, other)
    halo_ref[NS_ROWS + EW_ROWS :] = jnp.where(even, other, near)
    for here, start, row in ((GROUP - 1, NS_ROWS, 120), (0, NS_ROWS + EW_ROWS, 122)):
        for k, flag in ((0, 57), (1, 56)):
            flagged = (halo_ref[start + flag : start + flag + 1] == 1) & (place == here)
            old = halo_ref[row + k : row + k + 1]
            halo_ref[row + k : row + k + 1] = jnp.where(flagged, back_ref[3 + k : 4 + k], old)
    halo = halo_ref[...]
    flags = [flip_ref[0, k] for k in range(4)]
    north_e = jnp.where(flags[N_] == 1, cell(LAST, 0), cell(LAST, LAST))
    north_w = jnp.where(flags[N_] == 1, cell(LAST, LAST), cell(LAST, 0))
    south_e = jnp.where(flags[S_] == 1, cell(0, 0), cell(0, LAST))
    south_w = jnp.where(flags[S_] == 1, cell(0, LAST), cell(0, 0))
    far_e = arrived_ref[124:125, 0:1] == 1
    far_w = arrived_ref[125:126, 0:1] == 1
    rows = lax.broadcasted_iota(jnp.int32, (halo.shape[0], 1), 0)
    target = jnp.full(rows.shape, -1, jnp.int32)
    for row, yes, no, far in (
        (NS_ROWS + 54, south_e, north_e, far_e),
        (NS_ROWS + 55, north_e, south_e, far_e),
        (NS_ROWS + EW_ROWS + 54, south_w, north_w, far_w),
        (NS_ROWS + EW_ROWS + 55, north_w, south_w, far_w),
    ):
        target = jnp.where(rows == row, jnp.where(far, yes, no), target)
    lane = lax.broadcasted_iota(jnp.int32, (halo.shape[0], CELLS), 1)
    corner = jnp.where(lane == target, 1.0, 0.0).astype(jnp.bfloat16)
    high, low = split(halo.T)
    operator = operator_ref[...]
    walks = dot(high, operator) + dot(low, operator)
    extra = dot(high, corner) + dot(low, corner)
    diffused = base_ref[...] + weighted(walks, rates) + rates * rates * rates * extra
    high, low = split(diffused)
    mix = dot(high_ref[...], high) + dot(high_ref[...], low) + dot(low_ref[...], high)
    total = jnp.zeros((level_count, CELLS), jnp.float32)
    for k in range(member_count):
        rows = slice(k * level_count, (k + 1) * level_count)
        total = total + perts_ref[k].astype(jnp.float32) * mix[rows]
    term_ref[...] = (gain_ref[...] * total).reshape(term_ref.shape)


def halo_rows():
    by_flag = [np.zeros((NS_ROWS + 2 * EW_ROWS, PASSES * CELLS), np.float32) for _ in range(2)]
    edge = np.full((NS_ROWS + 2 * EW_ROWS, 8), -1, np.int32)

    def put(row, zero, one=None, which=-1):
        by_flag[0][row] = WALKS[PLACE[zero]]
        by_flag[1][row] = WALKS[PLACE[one or zero]]
        edge[row] = which

    for a in range(PASSES):
        for i in range(SIDE):
            k = a * SIDE + i
            put(k, ("N", a, i))
            put(48 + k, ("S", a, i))
            put(NS_ROWS + k, ("E", a, i))
            put(NS_ROWS + EW_ROWS + k, ("W", a, i))
    for k, (a, b) in enumerate(CORNER):
        put(96 + k, ("NE", a, b), ("NW", a, b), N_)
        put(99 + k, ("SE", a, b), ("SW", a, b), S_)
        put(102 + k, ("NW", a, b), ("NE", a, b), N_)
        put(105 + k, ("SW", a, b), ("SE", a, b), S_)
        put(108 + k, ("EN", a, b), ("ES", a, b), E_)
        put(111 + k, ("ES", a, b), ("EN", a, b), E_)
        put(114 + k, ("WN", a, b), ("WS", a, b), W_)
        put(117 + k, ("WS", a, b), ("WN", a, b), W_)
    put(120, ("q", "EN"), ("q", "ES"), E_)
    put(121, ("q", "ES"), ("q", "EN"), E_)
    put(122, ("q", "WN"), ("q", "WS"), W_)
    put(123, ("q", "WS"), ("q", "WN"), W_)
    return by_flag[0], by_flag[1], edge


def vmem(count):
    return [pl.BlockSpec(memory_space=pltpu.VMEM)] * count


SMEM = pl.BlockSpec(memory_space=pltpu.SMEM)


def room(mebibytes):
    return pltpu.CompilerParams(vmem_limit_bytes=mebibytes * 2**20)


def local(control, perts, diffusivity, vertical, gain, edge_flip):
    member_count, level_count, cell_count = control.shape
    tile_count = lax.axis_size("tile")
    mem_count = lax.axis_size("mem")
    lanes = member_count * level_count
    west_table, east_table, ns_table, q_table = pack_cells()

    place = (lax.axis_index("tile") % GROUP).astype(jnp.int32).reshape(1, 1)

    def exchanged(value, pairs):
        both = [(i % tile_count, j % tile_count) for i, j in pairs]
        return lax.ppermute(value, "tile", both + [(j, i) for i, j in both])

    def swapped(value, mask):
        return lax.ppermute(value, "tile", [(i, i ^ mask) for i in range(tile_count)])

    half = tile_count // 2
    edges = range(GROUP, tile_count + 1, GROUP)
    pairs = [(i, i + 1) for i in range(0, tile_count, 2)]
    between = [(i, i + 1) for i in range(1, tile_count, 2) if (i + 1) % GROUP]

    def rows_of(count):
        return jax.ShapeDtypeStruct((count, lanes), jnp.float32)

    table = table_columns(west_table + east_table + ns_table + q_table + [(0, 0, -1)] * 4)
    first, second, wrap, strips = pl.pallas_call(
        pack_kernel,
        out_shape=[rows_of(count) for count in (EW_ROWS, EW_ROWS, EW_ROWS, 104)],
        in_specs=vmem(1) + [SMEM, SMEM] + vmem(1),
        out_specs=vmem(4),
        name="packs",
    )(control, edge_flip, place, jnp.asarray(table))
    wrap = exchanged(wrap, [(k - 1, k) for k in edges] + [(k - 2, k + 1 + half) for k in edges])
    near = exchanged(first, pairs)
    control_there, first = lax.optimization_barrier((control, first))
    zero, one, edge = halo_rows()
    spread = diffusivity.reshape(1, level_count)
    wide = PASSES * cell_count
    base, operator, high, low = pl.pallas_call(
        own_kernel,
        out_shape=[
            jax.ShapeDtypeStruct((lanes, cell_count), jnp.float32),
            jax.ShapeDtypeStruct((NS_ROWS + 2 * EW_ROWS, wide), jnp.bfloat16),
            jax.ShapeDtypeStruct((lanes, lanes), jnp.bfloat16),
            jax.ShapeDtypeStruct((lanes, lanes), jnp.bfloat16),
        ],
        in_specs=vmem(3) + [SMEM] + vmem(4),
        out_specs=vmem(4),
        name="own_cells",
    )(
        control_there,
        spread,
        vertical,
        edge_flip,
        jnp.asarray(WALKS_OWN, jnp.bfloat16),
        jnp.asarray(zero, jnp.bfloat16),
        jnp.asarray(one, jnp.bfloat16),
        jnp.asarray(edge),
    )
    near, base = lax.optimization_barrier((near, base))
    second = pl.pallas_call(
        second_kernel, out_shape=rows_of(EW_ROWS), in_specs=vmem(2), out_specs=vmem(1)[0], name="second", compiler_params=room(4)
    )(second, near)
    other = exchanged(second, between)
    back = pl.pallas_call(
        third_kernel, out_shape=rows_of(8), in_specs=vmem(3) + [SMEM], out_specs=vmem(1)[0], name="third", compiler_params=room(4)
    )(second, other, wrap, place)
    back = exchanged(back, pairs)
    ns_pack, sums = pl.pallas_call(
        relay_kernel,
        out_shape=[rows_of(NS_ROWS), rows_of(16)],
        in_specs=vmem(6) + [SMEM],
        out_specs=vmem(2),
        name="relay", compiler_params=room(4),
    )(strips, second, near, other, wrap, back, place)
    arrived = exchanged(ns_pack, [(i, i + half) for i in range(half)])
    groups = [list(range(low_bits, tile_count, 4)) for low_bits in range(4)]
    sums = lax.all_to_all(sums, "tile", 0, 0, tiled=True, axis_index_groups=groups)
    pieces = pl.pallas_call(
        final_kernel,
        out_shape=jax.ShapeDtypeStruct((mem_count, level_count // mem_count, cell_count), jnp.float32),
        in_specs=vmem(10) + [SMEM, SMEM] + vmem(2),
        out_specs=vmem(1)[0],
        scratch_shapes=[pltpu.VMEM((NS_ROWS + 2 * EW_ROWS, lanes), jnp.float32)],
        name="localized",
                cost_estimate=pl.CostEstimate(flops=3450000000, bytes_accessed=1000000, transcendentals=0),
    )(
        base, operator, high, low, arrived, near, other, wrap, back,
        spread, edge_flip, place, perts, gain,
    )
    sums, pieces = lax.optimization_barrier((sums, pieces))
    pieces = lax.all_to_all(pieces, "mem", 0, 0, tiled=True)
    members_all = member_count * mem_count
    increment = jnp.sum(pieces, axis=0) / jnp.sqrt(jnp.float32(members_all - 1))
    norm_count = level_count * cell_count * tile_count
    sums = jnp.sum(sums.reshape(16, member_count, level_count), axis=(0, 2))
    member_cost = 0.5 * sums / norm_count
    return (increment, member_cost)


def solution(mesh):
    placed = (
        P("mem", None, "tile"),
        P("mem", None, "tile"),
        P(),
        P(),
        P(None, "tile"),
        P("tile", None),
    )
    return jax.shard_map(
        local, mesh=mesh, in_specs=placed, out_specs=(P("mem", "tile"), P("mem")), check_vma=False
    )
```

```python
import jax
import jax.numpy as jnp
import numpy as np
from jax import lax
from jax.experimental import pallas as pl
from jax.experimental.pallas import tpu as pltpu
from jax.sharding import PartitionSpec as P

PASSES = 3
SIDE = 16
CELLS = SIDE * SIDE
CORNER = ((0, 0), (0, 1), (1, 0))
LAST = SIDE - 1

EW_ROWS = 64
NS_ROWS = 128
GROUP = 16
S_, E_, N_, W_ = range(4)


def cell(row, col):
    return row * SIDE + col


def walk_operators():
    names = [("own", i, j) for i in range(SIDE) for j in range(SIDE)]
    for side in "EWNS":
        names += [(side, a, i) for a in range(PASSES) for i in range(SIDE)]
    ends = ("EN", "ES", "WN", "WS", "NE", "NW", "SE", "SW")
    for end in ends:
        names += [(end, a, b) for a, b in CORNER]
    names += [("q", end) for end in ends]
    place = {name: k for k, name in enumerate(names)}
    size = len(names)
    lap = np.zeros((size, size), np.int64)

    def link(name, others):
        row = place[name]
        lap[row, row] -= 4
        for other in others:
            lap[row, place[other]] += 1

    def inside(i, j):
        if i < 0:
            return ("S", -1 - i, j)
        if i > LAST:
            return ("N", i - SIDE, j)
        if j < 0:
            return ("W", -1 - j, i)
        if j > LAST:
            return ("E", j - SIDE, i)
        return ("own", i, j)

    for i in range(SIDE):
        for j in range(SIDE):
            link(("own", i, j), [inside(i + 1, j), inside(i - 1, j), inside(i, j + 1), inside(i, j - 1)])
    border = {
        "E": lambda i: ("own", i, LAST),
        "W": lambda i: ("own", i, 0),
        "N": lambda j: ("own", LAST, j),
        "S": lambda j: ("own", 0, j),
    }
    beyond = {"E": ("EN", "ES"), "W": ("WN", "WS"), "N": ("NE", "NW"), "S": ("SE", "SW")}
    for side in "EWNS":
        high, low = beyond[side]
        for a in range(PASSES - 1):
            for i in range(SIDE):
                link(
                    (side, a, i),
                    [
                        border[side](i) if a == 0 else (side, a - 1, i),
                        (side, a + 1, i),
                        (side, a, i + 1) if i < LAST else (high, a, 0),
                        (side, a, i - 1) if i > 0 else (low, a, 0),
                    ],
                )
        for end, last in ((high, LAST), (low, 0)):
            link((end, 0, 0), [(side, 0, last), (end, 1, 0), (end, 0, 1), ("q", end)])
    powers = [lap[:CELLS]]
    for _ in range(PASSES - 1):
        powers.append(powers[-1] @ lap)
    return place, np.concatenate([p.T for p in powers], axis=1).astype(np.float32)


PLACE, WALKS = walk_operators()
WALKS_OWN = WALKS[:CELLS]


def pack_cells():
    west, east, far = [], [], []
    for a in range(PASSES):
        for i in range(SIDE):
            west.append((cell(i, a), cell(LAST - i, a), W_))
            east.append((cell(i, LAST - a), cell(LAST - i, LAST - a), E_))
    for a, b in CORNER:
        west.append((cell(b, a), cell(b, LAST - a), S_))
        east.append((cell(b, LAST - a), cell(b, a), S_))
    for a, b in CORNER:
        west.append((cell(LAST - b, a), cell(LAST - b, LAST - a), N_))
        east.append((cell(LAST - b, LAST - a), cell(LAST - b, a), N_))
    west += [(cell(LAST, 0), cell(LAST, LAST), N_), (cell(0, 0), cell(0, LAST), S_)]
    east += [(cell(LAST, LAST), cell(LAST, 0), N_), (cell(0, LAST), cell(0, 0), S_)]
    north_south = []
    for a in range(PASSES):
        for j in range(SIDE):
            north_south.append((cell(a, j), cell(a, LAST - j), S_))
    for a in range(PASSES):
        for j in range(SIDE):
            north_south.append((cell(LAST - a, j), cell(LAST - a, LAST - j), N_))
    own_q = [
        (cell(0, LAST), cell(LAST, LAST), E_),
        (cell(LAST, LAST), cell(0, LAST), E_),
        (cell(0, 0), cell(LAST, 0), W_),
        (cell(LAST, 0), cell(0, 0), W_),
    ]
    return west, east, north_south, own_q


def split(value):
    high = value.astype(jnp.bfloat16)
    return high, (value - high.astype(jnp.float32)).astype(jnp.bfloat16)


def dot(left, right, dims=((1,), (0,))):
    return lax.dot_general(left, right, (dims, ((), ())), preferred_element_type=jnp.float32)


def table_columns(table):
    rows = np.zeros((len(table), 8), np.int32)
    rows[:, :3] = np.array(table, np.int32)
    return rows


def per_row(edge, flags, shape):
    flag = jnp.zeros(shape, jnp.int32)
    for k in range(4):
        flag = jnp.where(edge == k, flags[k], flag)
    return flag


def pack_kernel(field_ref, flip_ref, place_ref, table_ref, first_ref, second_ref, wrap_ref, strips_ref):
    field = field_ref[...].reshape(-1, CELLS)
    lanes = field.shape[0]
    flags = [flip_ref[0, k] for k in range(4)]
    edge = table_ref[:, 2:3]
    flag = per_row(edge, flags, edge.shape)
    index = jnp.where(flag == 1, table_ref[:, 1:2], table_ref[:, 0:1])
    lane = lax.broadcasted_iota(jnp.int32, (edge.shape[0], CELLS), 1)
    chosen = jnp.where(lane == index, 1.0, 0.0).astype(jnp.bfloat16)
    high, low = split(field)
    nt = ((1,), (1,))
    rows = dot(chosen, high, nt) + dot(chosen, low, nt)
    high, low = split(field * field)
    ones = jnp.ones((8, CELLS), jnp.bfloat16)
    norms = (dot(ones, high, nt) + dot(ones, low, nt))[0:1]
    level = [jnp.full((1, lanes), flags[k].astype(jnp.float32)) for k in range(4)]
    west, east = rows[0:56], rows[56:112]
    even = place_ref[0, 0] % 2 == 0
    first_ref[0:56] = jnp.where(even, east, west)
    second_ref[0:56] = jnp.where(even, west, east)
    for ref in (first_ref, second_ref):
        ref[56:57] = level[S_]
        ref[57:58] = level[N_]
        ref[58:59] = norms
        ref[59:64] = jnp.zeros((5, lanes), jnp.float32)
    at_end = (place_ref[0, 0] == 0) | (place_ref[0, 0] == GROUP - 1)
    wrap_ref[...] = jnp.where(at_end, second_ref[...], first_ref[...])
    strips_ref[0:100] = rows[112:212]
    strips_ref[100:101] = level[E_]
    strips_ref[101:102] = level[W_]
    strips_ref[102:103] = norms
    strips_ref[103:104] = jnp.zeros((1, lanes), jnp.float32)


def second_kernel(second_ref, near_ref, out_ref):
    out_ref[0:59] = second_ref[0:59]
    out_ref[59:60] = near_ref[0:1]
    out_ref[60:61] = near_ref[LAST : LAST + 1]
    out_ref[61:62] = second_ref[58:59] + near_ref[58:59]
    out_ref[62:64] = jnp.zeros((2, out_ref.shape[1]), jnp.float32)


def across(place, other, wrap):
    return jnp.where((place == 0) | (place == GROUP - 1), wrap, other)


def third_kernel(second_ref, other_ref, wrap_ref, place_ref, out_ref):
    place = place_ref[0, 0]
    out_ref[0:1] = across(place, other_ref[0:1], wrap_ref[0:1])
    out_ref[1:2] = across(place, other_ref[LAST : LAST + 1], wrap_ref[LAST : LAST + 1])
    out_ref[2:3] = second_ref[61:62] + other_ref[61:62]
    out_ref[3:4] = wrap_ref[0:1]
    out_ref[4:5] = wrap_ref[LAST : LAST + 1]
    out_ref[5:8] = jnp.zeros((3, out_ref.shape[1]), jnp.float32)


def relay_kernel(strips_ref, second_ref, near_ref, other_ref, wrap_ref, back_ref, place_ref, out_ref, sums_ref):
    place = place_ref[0, 0]
    even = place % 2 == 0
    near = near_ref[...]
    other = across(place, other_ref[...], wrap_ref[...])
    out_ref[0:96] = strips_ref[0:96]
    row = 96
    for pack, far in (
        (jnp.where(even, near, other), jnp.where(even, back_ref[0:2], other[59:61])),
        (jnp.where(even, other, near), jnp.where(even, other[59:61], back_ref[0:2])),
    ):
        side = (row - 96) // 6
        for a, b in CORNER:
            out_ref[row : row + 1] = pack[b * SIDE + a : b * SIDE + a + 1]
            out_ref[row + 3 : row + 4] = pack[b * SIDE + LAST - a : b * SIDE + SIDE - a]
            row += 1
        row += 3
        out_ref[108 + 6 * side : 114 + 6 * side] = pack[48:54]
        own = strips_ref[96 + 2 * side : 98 + 2 * side]
        out_ref[120 + 2 * side : 122 + 2 * side] = jnp.where(pack[56:58] == 1, far, own)
    out_ref[124:126] = strips_ref[100:102]
    y = place % 4
    sums = jnp.where((y == 1) | (y == 2), second_ref[61:62] + other[61:62], back_ref[2:3])
    out_ref[126:128] = jnp.zeros((2, out_ref.shape[1]), jnp.float32)
    sums_ref[...] = jnp.broadcast_to(sums[None], sums_ref.shape)


def rate_column(diffusivity_ref, member_count):
    levels = diffusivity_ref.shape[1]
    here = lax.broadcasted_iota(jnp.int32, (levels, levels), 0)
    there = lax.broadcasted_iota(jnp.int32, (levels, levels), 1)
    column = jnp.sum(jnp.where(here == there, diffusivity_ref[...], 0.0), axis=1, keepdims=True)
    return jnp.concatenate([column] * member_count, axis=0)


def weighted(walks, rates):
    one, two, three = (walks[:, k * CELLS : (k + 1) * CELLS] for k in range(PASSES))
    return rates * (3.0 * one + rates * (3.0 * two + rates * three))


def own_kernel(
    field_ref, diffusivity_ref, vertical_ref, flip_ref, walks_ref, zero_ref, one_ref, edge_ref,
    base_ref, operator_ref, high_ref, low_ref,
):
    member_count, level_count, _ = field_ref.shape
    field = field_ref[...].reshape(-1, CELLS)
    rates = rate_column(diffusivity_ref, member_count)
    high, low = split(field)
    walks = dot(high, walks_ref[...]) + dot(low, walks_ref[...])
    base_ref[...] = field + weighted(walks, rates)
    flags = [flip_ref[0, k] for k in range(4)]
    flag = per_row(edge_ref[:, 0:1], flags, (edge_ref.shape[0], 1))
    flag = jnp.broadcast_to(flag, zero_ref.shape) == 1
    operator_ref[...] = jnp.where(
        flag, one_ref[...].astype(jnp.float32), zero_ref[...].astype(jnp.float32)
    ).astype(jnp.bfloat16)
    lanes = member_count * level_count
    across = jnp.concatenate([vertical_ref[...]] * member_count, axis=1)
    whole = jnp.concatenate([across] * member_count, axis=0)
    here = lax.broadcasted_iota(jnp.int32, (lanes, lanes), 0) // level_count
    there = lax.broadcasted_iota(jnp.int32, (lanes, lanes), 1) // level_count
    high, low = split(jnp.where(here == there, whole, 0.0))
    high_ref[...] = high
    low_ref[...] = low

def final_kernel(
    base_ref, operator_ref, high_ref, low_ref, arrived_ref, near_ref, other_ref, wrap_ref, back_ref,
    diffusivity_ref, flip_ref, place_ref, perts_ref, gain_ref, term_ref,
    halo_ref,
):
    member_count, level_count, _ = perts_ref.shape
    rates = rate_column(diffusivity_ref, member_count)
    place = place_ref[0, 0]
    even = place % 2 == 0
    near = near_ref[...]
    other = across(place, other_ref[...], wrap_ref[...])
    halo_ref[0:NS_ROWS] = arrived_ref[...]
    halo_ref[NS_ROWS : NS_ROWS + EW_ROWS] = jnp.where(even, near, other)
    halo_ref[NS_ROWS + EW_ROWS :] = jnp.where(even, other, near)
    for here, start, row in ((GROUP - 1, NS_ROWS, 120), (0, NS_ROWS + EW_ROWS, 122)):
        for k, flag in ((0, 57), (1, 56)):
            flagged = (halo_ref[start + flag : start + flag + 1] == 1) & (place == here)
            old = halo_ref[row + k : row + k + 1]
            halo_ref[row + k : row + k + 1] = jnp.where(flagged, back_ref[3 + k : 4 + k], old)
    halo = halo_ref[...]
    flags = [flip_ref[0, k] for k in range(4)]
    north_e = jnp.where(flags[N_] == 1, cell(LAST, 0), cell(LAST, LAST))
    north_w = jnp.where(flags[N_] == 1, cell(LAST, LAST), cell(LAST, 0))
    south_e = jnp.where(flags[S_] == 1, cell(0, 0), cell(0, LAST))
    south_w = jnp.where(flags[S_] == 1, cell(0, LAST), cell(0, 0))
    far_e = arrived_ref[124:125, 0:1] == 1
    far_w = arrived_ref[125:126, 0:1] == 1
    rows = lax.broadcasted_iota(jnp.int32, (halo.shape[0], 1), 0)
    target = jnp.full(rows.shape, -1, jnp.int32)
    for row, yes, no, far in (
        (NS_ROWS + 54, south_e, north_e, far_e),
        (NS_ROWS + 55, north_e, south_e, far_e),
        (NS_ROWS + EW_ROWS + 54, south_w, north_w, far_w),
        (NS_ROWS + EW_ROWS + 55, north_w, south_w, far_w),
    ):
        target = jnp.where(rows == row, jnp.where(far, yes, no), target)
    lane = lax.broadcasted_iota(jnp.int32, (halo.shape[0], CELLS), 1)
    corner = jnp.where(lane == target, 1.0, 0.0).astype(jnp.bfloat16)
    high, low = split(halo.T)
    operator = operator_ref[...]
    walks = dot(high, operator) + dot(low, operator)
    extra = dot(high, corner) + dot(low, corner)
    diffused = base_ref[...] + weighted(walks, rates) + rates * rates * rates * extra
    high, low = split(diffused)
    mix = dot(high_ref[...], high) + dot(high_ref[...], low) + dot(low_ref[...], high)
    total = jnp.zeros((level_count, CELLS), jnp.float32)
    for k in range(member_count):
        rows = slice(k * level_count, (k + 1) * level_count)
        total = total + perts_ref[k].astype(jnp.float32) * mix[rows]
    term_ref[...] = (gain_ref[...] * total).reshape(term_ref.shape)


def halo_rows():
    by_flag = [np.zeros((NS_ROWS + 2 * EW_ROWS, PASSES * CELLS), np.float32) for _ in range(2)]
    edge = np.full((NS_ROWS + 2 * EW_ROWS, 8), -1, np.int32)

    def put(row, zero, one=None, which=-1):
        by_flag[0][row] = WALKS[PLACE[zero]]
        by_flag[1][row] = WALKS[PLACE[one or zero]]
        edge[row] = which

    for a in range(PASSES):
        for i in range(SIDE):
            k = a * SIDE + i
            put(k, ("N", a, i))
            put(48 + k, ("S", a, i))
            put(NS_ROWS + k, ("E", a, i))
            put(NS_ROWS + EW_ROWS + k, ("W", a, i))
    for k, (a, b) in enumerate(CORNER):
        put(96 + k, ("NE", a, b), ("NW", a, b), N_)
        put(99 + k, ("SE", a, b), ("SW", a, b), S_)
        put(102 + k, ("NW", a, b), ("NE", a, b), N_)
        put(105 + k, ("SW", a, b), ("SE", a, b), S_)
        put(108 + k, ("EN", a, b), ("ES", a, b), E_)
        put(111 + k, ("ES", a, b), ("EN", a, b), E_)
        put(114 + k, ("WN", a, b), ("WS", a, b), W_)
        put(117 + k, ("WS", a, b), ("WN", a, b), W_)
    put(120, ("q", "EN"), ("q", "ES"), E_)
    put(121, ("q", "ES"), ("q", "EN"), E_)
    put(122, ("q", "WN"), ("q", "WS"), W_)
    put(123, ("q", "WS"), ("q", "WN"), W_)
    return by_flag[0], by_flag[1], edge


def vmem(count):
    return [pl.BlockSpec(memory_space=pltpu.VMEM)] * count


SMEM = pl.BlockSpec(memory_space=pltpu.SMEM)


def room(mebibytes):
    return pltpu.CompilerParams(vmem_limit_bytes=mebibytes * 2**20)


def local(control, perts, diffusivity, vertical, gain, edge_flip):
    member_count, level_count, cell_count = control.shape
    tile_count = lax.axis_size("tile")
    mem_count = lax.axis_size("mem")
    lanes = member_count * level_count
    west_table, east_table, ns_table, q_table = pack_cells()

    place = (lax.axis_index("tile") % GROUP).astype(jnp.int32).reshape(1, 1)

    def exchanged(value, pairs):
        both = [(i % tile_count, j % tile_count) for i, j in pairs]
        return lax.ppermute(value, "tile", both + [(j, i) for i, j in both])

    def swapped(value, mask):
        return lax.ppermute(value, "tile", [(i, i ^ mask) for i in range(tile_count)])

    half = tile_count // 2
    edges = range(GROUP, tile_count + 1, GROUP)
    pairs = [(i, i + 1) for i in range(0, tile_count, 2)]
    between = [(i, i + 1) for i in range(1, tile_count, 2) if (i + 1) % GROUP]

    def rows_of(count):
        return jax.ShapeDtypeStruct((count, lanes), jnp.float32)

    table = table_columns(west_table + east_table + ns_table + q_table + [(0, 0, -1)] * 4)
    first, second, wrap, strips = pl.pallas_call(
        pack_kernel,
        out_shape=[rows_of(count) for count in (EW_ROWS, EW_ROWS, EW_ROWS, 104)],
        in_specs=vmem(1) + [SMEM, SMEM] + vmem(1),
        out_specs=vmem(4),
        name="packs",
    )(control, edge_flip, place, jnp.asarray(table))
    wrap = exchanged(wrap, [(k - 1, k) for k in edges] + [(k - 2, k + 1 + half) for k in edges])
    near = exchanged(first, pairs)
    control_there, first = lax.optimization_barrier((control, first))
    zero, one, edge = halo_rows()
    spread = diffusivity.reshape(1, level_count)
    wide = PASSES * cell_count
    base, operator, high, low = pl.pallas_call(
        own_kernel,
        out_shape=[
            jax.ShapeDtypeStruct((lanes, cell_count), jnp.float32),
            jax.ShapeDtypeStruct((NS_ROWS + 2 * EW_ROWS, wide), jnp.bfloat16),
            jax.ShapeDtypeStruct((lanes, lanes), jnp.bfloat16),
            jax.ShapeDtypeStruct((lanes, lanes), jnp.bfloat16),
        ],
        in_specs=vmem(3) + [SMEM] + vmem(4),
        out_specs=vmem(4),
        name="own_cells",
    )(
        control_there,
        spread,
        vertical,
        edge_flip,
        jnp.asarray(WALKS_OWN, jnp.bfloat16),
        jnp.asarray(zero, jnp.bfloat16),
        jnp.asarray(one, jnp.bfloat16),
        jnp.asarray(edge),
    )
    near, base = lax.optimization_barrier((near, base))
    second = pl.pallas_call(
        second_kernel, out_shape=rows_of(EW_ROWS), in_specs=vmem(2), out_specs=vmem(1)[0], name="second", compiler_params=room(4)
    )(second, near)
    other = exchanged(second, between)
    back = pl.pallas_call(
        third_kernel, out_shape=rows_of(8), in_specs=vmem(3) + [SMEM], out_specs=vmem(1)[0], name="third", compiler_params=room(4)
    )(second, other, wrap, place)
    back = exchanged(back, pairs)
    ns_pack, sums = pl.pallas_call(
        relay_kernel,
        out_shape=[rows_of(NS_ROWS), jax.ShapeDtypeStruct((GROUP, 1, lanes), jnp.float32)],
        in_specs=vmem(6) + [SMEM],
        out_specs=vmem(2),
        name="relay", compiler_params=room(4),
    )(strips, second, near, other, wrap, back, place)
    arrived = exchanged(ns_pack, [(i, i + half) for i in range(half)])
    groups = [list(range(low_bits, tile_count, 4)) for low_bits in range(4)]
    sums = lax.all_to_all(sums, "tile", 0, 0, tiled=True, axis_index_groups=groups)
    pieces = pl.pallas_call(
        final_kernel,
        out_shape=jax.ShapeDtypeStruct((mem_count, level_count // mem_count, cell_count), jnp.float32),
        in_specs=vmem(10) + [SMEM, SMEM] + vmem(2),
        out_specs=vmem(1)[0],
        scratch_shapes=[pltpu.VMEM((NS_ROWS + 2 * EW_ROWS, lanes), jnp.float32)],
        name="localized",
                cost_estimate=pl.CostEstimate(flops=11499999999, bytes_accessed=1000000, transcendentals=0),
    )(
        base, operator, high, low, arrived, near, other, wrap, back,
        spread, edge_flip, place, perts, gain,
    )
    sums, pieces = lax.optimization_barrier((sums, pieces))
    pieces = lax.all_to_all(pieces, "mem", 0, 0, tiled=True)
    members_all = member_count * mem_count
    increment = jnp.sum(pieces, axis=0) / jnp.sqrt(jnp.float32(members_all - 1))
    norm_count = level_count * cell_count * tile_count
    sums = jnp.sum(sums[:, 0].reshape(GROUP, member_count, level_count), axis=(0, 2))
    member_cost = 0.5 * sums / norm_count
    return (increment, member_cost)


def solution(mesh):
    placed = (
        P("mem", None, "tile"),
        P("mem", None, "tile"),
        P(),
        P(),
        P(None, "tile"),
        P("tile", None),
    )
    return jax.shard_map(
        local, mesh=mesh, in_specs=placed, out_specs=(P("mem", "tile"), P("mem")), check_vma=False
    )
```

```python
import jax
import jax.numpy as jnp
import numpy as np
from jax import lax
from jax.experimental import pallas as pl
from jax.experimental.pallas import tpu as pltpu
from jax.sharding import PartitionSpec as P

PASSES = 3
SIDE = 16
CELLS = SIDE * SIDE
CORNER = ((0, 0), (0, 1), (1, 0))
LAST = SIDE - 1

EW_ROWS = 64
NS_ROWS = 128
GROUP = 16
S_, E_, N_, W_ = range(4)


def cell(row, col):
    return row * SIDE + col


def walk_operators():
    names = [("own", i, j) for i in range(SIDE) for j in range(SIDE)]
    for side in "EWNS":
        names += [(side, a, i) for a in range(PASSES) for i in range(SIDE)]
    ends = ("EN", "ES", "WN", "WS", "NE", "NW", "SE", "SW")
    for end in ends:
        names += [(end, a, b) for a, b in CORNER]
    names += [("q", end) for end in ends]
    place = {name: k for k, name in enumerate(names)}
    size = len(names)
    lap = np.zeros((size, size), np.int64)

    def link(name, others):
        row = place[name]
        lap[row, row] -= 4
        for other in others:
            lap[row, place[other]] += 1

    def inside(i, j):
        if i < 0:
            return ("S", -1 - i, j)
        if i > LAST:
            return ("N", i - SIDE, j)
        if j < 0:
            return ("W", -1 - j, i)
        if j > LAST:
            return ("E", j - SIDE, i)
        return ("own", i, j)

    for i in range(SIDE):
        for j in range(SIDE):
            link(("own", i, j), [inside(i + 1, j), inside(i - 1, j), inside(i, j + 1), inside(i, j - 1)])
    border = {
        "E": lambda i: ("own", i, LAST),
        "W": lambda i: ("own", i, 0),
        "N": lambda j: ("own", LAST, j),
        "S": lambda j: ("own", 0, j),
    }
    beyond = {"E": ("EN", "ES"), "W": ("WN", "WS"), "N": ("NE", "NW"), "S": ("SE", "SW")}
    for side in "EWNS":
        high, low = beyond[side]
        for a in range(PASSES - 1):
            for i in range(SIDE):
                link(
                    (side, a, i),
                    [
                        border[side](i) if a == 0 else (side, a - 1, i),
                        (side, a + 1, i),
                        (side, a, i + 1) if i < LAST else (high, a, 0),
                        (side, a, i - 1) if i > 0 else (low, a, 0),
                    ],
                )
        for end, last in ((high, LAST), (low, 0)):
            link((end, 0, 0), [(side, 0, last), (end, 1, 0), (end, 0, 1), ("q", end)])
    powers = [lap[:CELLS]]
    for _ in range(PASSES - 1):
        powers.append(powers[-1] @ lap)
    return place, np.concatenate([p.T for p in powers], axis=1).astype(np.float32)


PLACE, WALKS = walk_operators()
WALKS_OWN = WALKS[:CELLS]


def pack_cells():
    west, east, far = [], [], []
    for a in range(PASSES):
        for i in range(SIDE):
            west.append((cell(i, a), cell(LAST - i, a), W_))
            east.append((cell(i, LAST - a), cell(LAST - i, LAST - a), E_))
    for a, b in CORNER:
        west.append((cell(b, a), cell(b, LAST - a), S_))
        east.append((cell(b, LAST - a), cell(b, a), S_))
    for a, b in CORNER:
        west.append((cell(LAST - b, a), cell(LAST - b, LAST - a), N_))
        east.append((cell(LAST - b, LAST - a), cell(LAST - b, a), N_))
    west += [(cell(LAST, 0), cell(LAST, LAST), N_), (cell(0, 0), cell(0, LAST), S_)]
    east += [(cell(LAST, LAST), cell(LAST, 0), N_), (cell(0, LAST), cell(0, 0), S_)]
    north_south = []
    for a in range(PASSES):
        for j in range(SIDE):
            north_south.append((cell(a, j), cell(a, LAST - j), S_))
    for a in range(PASSES):
        for j in range(SIDE):
            north_south.append((cell(LAST - a, j), cell(LAST - a, LAST - j), N_))
    own_q = [
        (cell(0, LAST), cell(LAST, LAST), E_),
        (cell(LAST, LAST), cell(0, LAST), E_),
        (cell(0, 0), cell(LAST, 0), W_),
        (cell(LAST, 0), cell(0, 0), W_),
    ]
    return west, east, north_south, own_q


def split(value):
    high = value.astype(jnp.bfloat16)
    return high, (value - high.astype(jnp.float32)).astype(jnp.bfloat16)


def dot(left, right, dims=((1,), (0,))):
    return lax.dot_general(left, right, (dims, ((), ())), preferred_element_type=jnp.float32)


def table_columns(table):
    rows = np.zeros((len(table), 8), np.int32)
    rows[:, :3] = np.array(table, np.int32)
    return rows


def per_row(edge, flags, shape):
    flag = jnp.zeros(shape, jnp.int32)
    for k in range(4):
        flag = jnp.where(edge == k, flags[k], flag)
    return flag


def pack_kernel(field_ref, flip_ref, place_ref, table_ref, first_ref, second_ref, wrap_ref, strips_ref):
    field = field_ref[...].reshape(-1, CELLS)
    lanes = field.shape[0]
    flags = [flip_ref[0, k] for k in range(4)]
    edge = table_ref[:, 2:3]
    flag = per_row(edge, flags, edge.shape)
    index = jnp.where(flag == 1, table_ref[:, 1:2], table_ref[:, 0:1])
    lane = lax.broadcasted_iota(jnp.int32, (edge.shape[0], CELLS), 1)
    chosen = jnp.where(lane == index, 1.0, 0.0).astype(jnp.bfloat16)
    high, low = split(field)
    nt = ((1,), (1,))
    rows = dot(chosen, high, nt) + dot(chosen, low, nt)
    high, low = split(field * field)
    ones = jnp.ones((8, CELLS), jnp.bfloat16)
    norms = (dot(ones, high, nt) + dot(ones, low, nt))[0:1]
    level = [jnp.full((1, lanes), flags[k].astype(jnp.float32)) for k in range(4)]
    west, east = rows[0:56], rows[56:112]
    even = place_ref[0, 0] % 2 == 0
    first_ref[0:56] = jnp.where(even, east, west)
    second_ref[0:56] = jnp.where(even, west, east)
    for ref in (first_ref, second_ref):
        ref[56:57] = level[S_]
        ref[57:58] = level[N_]
        ref[58:59] = norms
        ref[59:64] = jnp.zeros((5, lanes), jnp.float32)
    at_end = (place_ref[0, 0] == 0) | (place_ref[0, 0] == GROUP - 1)
    wrap_ref[...] = jnp.where(at_end, second_ref[...], first_ref[...])
    strips_ref[0:100] = rows[112:212]
    strips_ref[100:101] = level[E_]
    strips_ref[101:102] = level[W_]
    strips_ref[102:103] = norms
    strips_ref[103:104] = jnp.zeros((1, lanes), jnp.float32)


def second_kernel(second_ref, near_ref, out_ref):
    out_ref[0:59] = second_ref[0:59]
    out_ref[59:60] = near_ref[0:1]
    out_ref[60:61] = near_ref[LAST : LAST + 1]
    out_ref[61:62] = second_ref[58:59] + near_ref[58:59]
    out_ref[62:64] = jnp.zeros((2, out_ref.shape[1]), jnp.float32)


def across(place, other, wrap):
    return jnp.where((place == 0) | (place == GROUP - 1), wrap, other)


def third_kernel(second_ref, other_ref, wrap_ref, place_ref, out_ref):
    place = place_ref[0, 0]
    out_ref[0:1] = across(place, other_ref[0:1], wrap_ref[0:1])
    out_ref[1:2] = across(place, other_ref[LAST : LAST + 1], wrap_ref[LAST : LAST + 1])
    out_ref[2:3] = second_ref[61:62] + other_ref[61:62]
    out_ref[3:4] = wrap_ref[0:1]
    out_ref[4:5] = wrap_ref[LAST : LAST + 1]
    out_ref[5:8] = jnp.zeros((3, out_ref.shape[1]), jnp.float32)


def relay_kernel(strips_ref, second_ref, near_ref, other_ref, wrap_ref, back_ref, place_ref, out_ref, sums_ref):
    place = place_ref[0, 0]
    even = place % 2 == 0
    near = near_ref[...]
    other = across(place, other_ref[...], wrap_ref[...])
    out_ref[0:96] = strips_ref[0:96]
    row = 96
    for pack, far in (
        (jnp.where(even, near, other), jnp.where(even, back_ref[0:2], other[59:61])),
        (jnp.where(even, other, near), jnp.where(even, other[59:61], back_ref[0:2])),
    ):
        side = (row - 96) // 6
        for a, b in CORNER:
            out_ref[row : row + 1] = pack[b * SIDE + a : b * SIDE + a + 1]
            out_ref[row + 3 : row + 4] = pack[b * SIDE + LAST - a : b * SIDE + SIDE - a]
            row += 1
        row += 3
        out_ref[108 + 6 * side : 114 + 6 * side] = pack[48:54]
        own = strips_ref[96 + 2 * side : 98 + 2 * side]
        out_ref[120 + 2 * side : 122 + 2 * side] = jnp.where(pack[56:58] == 1, far, own)
    out_ref[124:126] = strips_ref[100:102]
    y = place % 4
    sums = jnp.where((y == 1) | (y == 2), second_ref[61:62] + other[61:62], back_ref[2:3])
    out_ref[126:128] = jnp.zeros((2, out_ref.shape[1]), jnp.float32)
    sums_ref[...] = jnp.broadcast_to(sums[None], sums_ref.shape)


def rate_column(diffusivity_ref, member_count):
    levels = diffusivity_ref.shape[1]
    here = lax.broadcasted_iota(jnp.int32, (levels, levels), 0)
    there = lax.broadcasted_iota(jnp.int32, (levels, levels), 1)
    column = jnp.sum(jnp.where(here == there, diffusivity_ref[...], 0.0), axis=1, keepdims=True)
    return jnp.concatenate([column] * member_count, axis=0)


def weighted(walks, rates):
    one, two, three = (walks[:, k * CELLS : (k + 1) * CELLS] for k in range(PASSES))
    return rates * (3.0 * one + rates * (3.0 * two + rates * three))


def own_kernel(
    field_ref, diffusivity_ref, vertical_ref, flip_ref, walks_ref, zero_ref, one_ref, edge_ref,
    base_ref, operator_ref, high_ref, low_ref,
):
    member_count, level_count, _ = field_ref.shape
    field = field_ref[...].reshape(-1, CELLS)
    rates = rate_column(diffusivity_ref, member_count)
    high, low = split(field)
    walks = dot(high, walks_ref[...]) + dot(low, walks_ref[...])
    base_ref[...] = field + weighted(walks, rates)
    flags = [flip_ref[0, k] for k in range(4)]
    flag = per_row(edge_ref[:, 0:1], flags, (edge_ref.shape[0], 1))
    flag = jnp.broadcast_to(flag, zero_ref.shape) == 1
    operator_ref[...] = jnp.where(
        flag, one_ref[...].astype(jnp.float32), zero_ref[...].astype(jnp.float32)
    ).astype(jnp.bfloat16)
    lanes = member_count * level_count
    across = jnp.concatenate([vertical_ref[...]] * member_count, axis=1)
    whole = jnp.concatenate([across] * member_count, axis=0)
    here = lax.broadcasted_iota(jnp.int32, (lanes, lanes), 0) // level_count
    there = lax.broadcasted_iota(jnp.int32, (lanes, lanes), 1) // level_count
    high, low = split(jnp.where(here == there, whole, 0.0))
    high_ref[...] = high
    low_ref[...] = low

def final_kernel(
    base_ref, operator_ref, high_ref, low_ref, arrived_ref, near_ref, other_ref, wrap_ref, back_ref,
    diffusivity_ref, flip_ref, place_ref, perts_ref, gain_ref, term_ref,
    halo_ref,
):
    member_count, level_count, _ = perts_ref.shape
    rates = rate_column(diffusivity_ref, member_count)
    place = place_ref[0, 0]
    even = place % 2 == 0
    near = near_ref[...]
    other = across(place, other_ref[...], wrap_ref[...])
    halo_ref[0:NS_ROWS] = arrived_ref[...]
    halo_ref[NS_ROWS : NS_ROWS + EW_ROWS] = jnp.where(even, near, other)
    halo_ref[NS_ROWS + EW_ROWS :] = jnp.where(even, other, near)
    for here, start, row in ((GROUP - 1, NS_ROWS, 120), (0, NS_ROWS + EW_ROWS, 122)):
        for k, flag in ((0, 57), (1, 56)):
            flagged = (halo_ref[start + flag : start + flag + 1] == 1) & (place == here)
            old = halo_ref[row + k : row + k + 1]
            halo_ref[row + k : row + k + 1] = jnp.where(flagged, back_ref[3 + k : 4 + k], old)
    halo = halo_ref[...]
    flags = [flip_ref[0, k] for k in range(4)]
    north_e = jnp.where(flags[N_] == 1, cell(LAST, 0), cell(LAST, LAST))
    north_w = jnp.where(flags[N_] == 1, cell(LAST, LAST), cell(LAST, 0))
    south_e = jnp.where(flags[S_] == 1, cell(0, 0), cell(0, LAST))
    south_w = jnp.where(flags[S_] == 1, cell(0, LAST), cell(0, 0))
    far_e = arrived_ref[124:125, 0:1] == 1
    far_w = arrived_ref[125:126, 0:1] == 1
    rows = lax.broadcasted_iota(jnp.int32, (halo.shape[0], 1), 0)
    target = jnp.full(rows.shape, -1, jnp.int32)
    for row, yes, no, far in (
        (NS_ROWS + 54, south_e, north_e, far_e),
        (NS_ROWS + 55, north_e, south_e, far_e),
        (NS_ROWS + EW_ROWS + 54, south_w, north_w, far_w),
        (NS_ROWS + EW_ROWS + 55, north_w, south_w, far_w),
    ):
        target = jnp.where(rows == row, jnp.where(far, yes, no), target)
    lane = lax.broadcasted_iota(jnp.int32, (halo.shape[0], CELLS), 1)
    corner = jnp.where(lane == target, 1.0, 0.0).astype(jnp.bfloat16)
    high, low = split(halo.T)
    operator = operator_ref[...]
    walks = dot(high, operator) + dot(low, operator)
    extra = dot(high, corner) + dot(low, corner)
    diffused = base_ref[...] + weighted(walks, rates) + rates * rates * rates * extra
    high, low = split(diffused)
    mix = dot(high_ref[...], high) + dot(high_ref[...], low) + dot(low_ref[...], high)
    total = jnp.zeros((level_count, CELLS), jnp.float32)
    for k in range(member_count):
        rows = slice(k * level_count, (k + 1) * level_count)
        total = total + perts_ref[k].astype(jnp.float32) * mix[rows]
    term_ref[...] = (gain_ref[...] * total).reshape(term_ref.shape)


def halo_rows():
    by_flag = [np.zeros((NS_ROWS + 2 * EW_ROWS, PASSES * CELLS), np.float32) for _ in range(2)]
    edge = np.full((NS_ROWS + 2 * EW_ROWS, 8), -1, np.int32)

    def put(row, zero, one=None, which=-1):
        by_flag[0][row] = WALKS[PLACE[zero]]
        by_flag[1][row] = WALKS[PLACE[one or zero]]
        edge[row] = which

    for a in range(PASSES):
        for i in range(SIDE):
            k = a * SIDE + i
            put(k, ("N", a, i))
            put(48 + k, ("S", a, i))
            put(NS_ROWS + k, ("E", a, i))
            put(NS_ROWS + EW_ROWS + k, ("W", a, i))
    for k, (a, b) in enumerate(CORNER):
        put(96 + k, ("NE", a, b), ("NW", a, b), N_)
        put(99 + k, ("SE", a, b), ("SW", a, b), S_)
        put(102 + k, ("NW", a, b), ("NE", a, b), N_)
        put(105 + k, ("SW", a, b), ("SE", a, b), S_)
        put(108 + k, ("EN", a, b), ("ES", a, b), E_)
        put(111 + k, ("ES", a, b), ("EN", a, b), E_)
        put(114 + k, ("WN", a, b), ("WS", a, b), W_)
        put(117 + k, ("WS", a, b), ("WN", a, b), W_)
    put(120, ("q", "EN"), ("q", "ES"), E_)
    put(121, ("q", "ES"), ("q", "EN"), E_)
    put(122, ("q", "WN"), ("q", "WS"), W_)
    put(123, ("q", "WS"), ("q", "WN"), W_)
    return by_flag[0], by_flag[1], edge


def vmem(count):
    return [pl.BlockSpec(memory_space=pltpu.VMEM)] * count


SMEM = pl.BlockSpec(memory_space=pltpu.SMEM)


def room(mebibytes):
    return pltpu.CompilerParams(vmem_limit_bytes=mebibytes * 2**20)


def local(control, perts, diffusivity, vertical, gain, edge_flip):
    member_count, level_count, cell_count = control.shape
    tile_count = lax.axis_size("tile")
    mem_count = lax.axis_size("mem")
    lanes = member_count * level_count
    west_table, east_table, ns_table, q_table = pack_cells()

    place = (lax.axis_index("tile") % GROUP).astype(jnp.int32).reshape(1, 1)

    def exchanged(value, pairs):
        both = [(i % tile_count, j % tile_count) for i, j in pairs]
        return lax.ppermute(value, "tile", both + [(j, i) for i, j in both])

    def swapped(value, mask):
        return lax.ppermute(value, "tile", [(i, i ^ mask) for i in range(tile_count)])

    half = tile_count // 2
    edges = range(GROUP, tile_count + 1, GROUP)
    pairs = [(i, i + 1) for i in range(0, tile_count, 2)]
    between = [(i, i + 1) for i in range(1, tile_count, 2) if (i + 1) % GROUP]

    def rows_of(count):
        return jax.ShapeDtypeStruct((count, lanes), jnp.float32)

    table = table_columns(west_table + east_table + ns_table + q_table + [(0, 0, -1)] * 4)
    first, second, wrap, strips = pl.pallas_call(
        pack_kernel,
        out_shape=[rows_of(count) for count in (EW_ROWS, EW_ROWS, EW_ROWS, 104)],
        in_specs=vmem(1) + [SMEM, SMEM] + vmem(1),
        out_specs=vmem(4),
        name="packs",
    )(control, edge_flip, place, jnp.asarray(table))
    wrap = exchanged(wrap, [(k - 1, k) for k in edges] + [(k - 2, k + 1 + half) for k in edges])
    near = exchanged(first, pairs)
    second = pl.pallas_call(
        second_kernel, out_shape=rows_of(EW_ROWS), in_specs=vmem(2), out_specs=vmem(1)[0], name="second", compiler_params=room(4)
    )(second, near)
    other = exchanged(second, between)
    back = pl.pallas_call(
        third_kernel, out_shape=rows_of(8), in_specs=vmem(3) + [SMEM], out_specs=vmem(1)[0], name="third", compiler_params=room(4)
    )(second, other, wrap, place)
    back = exchanged(back, pairs)
    ns_pack, sums = pl.pallas_call(
        relay_kernel,
        out_shape=[rows_of(NS_ROWS), jax.ShapeDtypeStruct((GROUP, 1, lanes), jnp.float32)],
        in_specs=vmem(6) + [SMEM],
        out_specs=vmem(2),
        name="relay", compiler_params=room(4),
    )(strips, second, near, other, wrap, back, place)
    arrived = exchanged(ns_pack, [(i, i + half) for i in range(half)])
    control_there, ns_pack = lax.optimization_barrier((control, ns_pack))
    zero, one, edge = halo_rows()
    spread = diffusivity.reshape(1, level_count)
    wide = PASSES * cell_count
    base, operator, high, low = pl.pallas_call(
        own_kernel,
        out_shape=[
            jax.ShapeDtypeStruct((lanes, cell_count), jnp.float32),
            jax.ShapeDtypeStruct((NS_ROWS + 2 * EW_ROWS, wide), jnp.bfloat16),
            jax.ShapeDtypeStruct((lanes, lanes), jnp.bfloat16),
            jax.ShapeDtypeStruct((lanes, lanes), jnp.bfloat16),
        ],
        in_specs=vmem(3) + [SMEM] + vmem(4),
        out_specs=vmem(4),
        name="own_cells",
    )(
        control_there,
        spread,
        vertical,
        edge_flip,
        jnp.asarray(WALKS_OWN, jnp.bfloat16),
        jnp.asarray(zero, jnp.bfloat16),
        jnp.asarray(one, jnp.bfloat16),
        jnp.asarray(edge),
    )
    groups = [list(range(low_bits, tile_count, 4)) for low_bits in range(4)]
    sums = lax.all_to_all(sums, "tile", 0, 0, tiled=True, axis_index_groups=groups)
    pieces = pl.pallas_call(
        final_kernel,
        out_shape=jax.ShapeDtypeStruct((mem_count, level_count // mem_count, cell_count), jnp.float32),
        in_specs=vmem(10) + [SMEM, SMEM] + vmem(2),
        out_specs=vmem(1)[0],
        scratch_shapes=[pltpu.VMEM((NS_ROWS + 2 * EW_ROWS, lanes), jnp.float32)],
        name="localized",
                cost_estimate=pl.CostEstimate(flops=11499999999, bytes_accessed=1000000, transcendentals=0),
    )(
        base, operator, high, low, arrived, near, other, wrap, back,
        spread, edge_flip, place, perts, gain,
    )
    sums, pieces = lax.optimization_barrier((sums, pieces))
    pieces = lax.all_to_all(pieces, "mem", 0, 0, tiled=True)
    members_all = member_count * mem_count
    increment = jnp.sum(pieces, axis=0) / jnp.sqrt(jnp.float32(members_all - 1))
    norm_count = level_count * cell_count * tile_count
    sums = jnp.sum(sums[:, 0].reshape(GROUP, member_count, level_count), axis=(0, 2))
    member_cost = 0.5 * sums / norm_count
    return (increment, member_cost)


def solution(mesh):
    placed = (
        P("mem", None, "tile"),
        P("mem", None, "tile"),
        P(),
        P(),
        P(None, "tile"),
        P("tile", None),
    )
    return jax.shard_map(
        local, mesh=mesh, in_specs=placed, out_specs=(P("mem", "tile"), P("mem")), check_vma=False
    )
```

```python
import jax
import jax.numpy as jnp
import numpy as np
from jax import lax
from jax.experimental import pallas as pl
from jax.experimental.pallas import tpu as pltpu
from jax.sharding import PartitionSpec as P

PASSES = 3
SIDE = 16
CELLS = SIDE * SIDE
CORNER = ((0, 0), (0, 1), (1, 0))
LAST = SIDE - 1

EW_ROWS = 64
NS_ROWS = 128
GROUP = 16
S_, E_, N_, W_ = range(4)


def cell(row, col):
    return row * SIDE + col


def walk_operators():
    names = [("own", i, j) for i in range(SIDE) for j in range(SIDE)]
    for side in "EWNS":
        names += [(side, a, i) for a in range(PASSES) for i in range(SIDE)]
    ends = ("EN", "ES", "WN", "WS", "NE", "NW", "SE", "SW")
    for end in ends:
        names += [(end, a, b) for a, b in CORNER]
    names += [("q", end) for end in ends]
    place = {name: k for k, name in enumerate(names)}
    size = len(names)
    lap = np.zeros((size, size), np.int64)

    def link(name, others):
        row = place[name]
        lap[row, row] -= 4
        for other in others:
            lap[row, place[other]] += 1

    def inside(i, j):
        if i < 0:
            return ("S", -1 - i, j)
        if i > LAST:
            return ("N", i - SIDE, j)
        if j < 0:
            return ("W", -1 - j, i)
        if j > LAST:
            return ("E", j - SIDE, i)
        return ("own", i, j)

    for i in range(SIDE):
        for j in range(SIDE):
            link(("own", i, j), [inside(i + 1, j), inside(i - 1, j), inside(i, j + 1), inside(i, j - 1)])
    border = {
        "E": lambda i: ("own", i, LAST),
        "W": lambda i: ("own", i, 0),
        "N": lambda j: ("own", LAST, j),
        "S": lambda j: ("own", 0, j),
    }
    beyond = {"E": ("EN", "ES"), "W": ("WN", "WS"), "N": ("NE", "NW"), "S": ("SE", "SW")}
    for side in "EWNS":
        high, low = beyond[side]
        for a in range(PASSES - 1):
            for i in range(SIDE):
                link(
                    (side, a, i),
                    [
                        border[side](i) if a == 0 else (side, a - 1, i),
                        (side, a + 1, i),
                        (side, a, i + 1) if i < LAST else (high, a, 0),
                        (side, a, i - 1) if i > 0 else (low, a, 0),
                    ],
                )
        for end, last in ((high, LAST), (low, 0)):
            link((end, 0, 0), [(side, 0, last), (end, 1, 0), (end, 0, 1), ("q", end)])
    powers = [lap[:CELLS]]
    for _ in range(PASSES - 1):
        powers.append(powers[-1] @ lap)
    return place, np.concatenate([p.T for p in powers], axis=1).astype(np.float32)


PLACE, WALKS = walk_operators()
WALKS_OWN = WALKS[:CELLS]


def pack_cells():
    west, east, far = [], [], []
    for a in range(PASSES):
        for i in range(SIDE):
            west.append((cell(i, a), cell(LAST - i, a), W_))
            east.append((cell(i, LAST - a), cell(LAST - i, LAST - a), E_))
    for a, b in CORNER:
        west.append((cell(b, a), cell(b, LAST - a), S_))
        east.append((cell(b, LAST - a), cell(b, a), S_))
    for a, b in CORNER:
        west.append((cell(LAST - b, a), cell(LAST - b, LAST - a), N_))
        east.append((cell(LAST - b, LAST - a), cell(LAST - b, a), N_))
    west += [(cell(LAST, 0), cell(LAST, LAST), N_), (cell(0, 0), cell(0, LAST), S_)]
    east += [(cell(LAST, LAST), cell(LAST, 0), N_), (cell(0, LAST), cell(0, 0), S_)]
    north_south = []
    for a in range(PASSES):
        for j in range(SIDE):
            north_south.append((cell(a, j), cell(a, LAST - j), S_))
    for a in range(PASSES):
        for j in range(SIDE):
            north_south.append((cell(LAST - a, j), cell(LAST - a, LAST - j), N_))
    own_q = [
        (cell(0, LAST), cell(LAST, LAST), E_),
        (cell(LAST, LAST), cell(0, LAST), E_),
        (cell(0, 0), cell(LAST, 0), W_),
        (cell(LAST, 0), cell(0, 0), W_),
    ]
    return west, east, north_south, own_q


def split(value):
    high = value.astype(jnp.bfloat16)
    return high, (value - high.astype(jnp.float32)).astype(jnp.bfloat16)


def dot(left, right, dims=((1,), (0,))):
    return lax.dot_general(left, right, (dims, ((), ())), preferred_element_type=jnp.float32)


def table_columns(table):
    rows = np.zeros((len(table), 8), np.int32)
    rows[:, :3] = np.array(table, np.int32)
    return rows


def per_row(edge, flags, shape):
    flag = jnp.zeros(shape, jnp.int32)
    for k in range(4):
        flag = jnp.where(edge == k, flags[k], flag)
    return flag


def pack_kernel(field_ref, flip_ref, place_ref, table_ref, first_ref, second_ref, wrap_ref, strips_ref):
    field = field_ref[...].reshape(-1, CELLS)
    lanes = field.shape[0]
    flags = [flip_ref[0, k] for k in range(4)]
    edge = table_ref[:, 2:3]
    flag = per_row(edge, flags, edge.shape)
    index = jnp.where(flag == 1, table_ref[:, 1:2], table_ref[:, 0:1])
    lane = lax.broadcasted_iota(jnp.int32, (edge.shape[0], CELLS), 1)
    chosen = jnp.where(lane == index, 1.0, 0.0).astype(jnp.bfloat16)
    high, low = split(field)
    nt = ((1,), (1,))
    rows = dot(chosen, high, nt) + dot(chosen, low, nt)
    high, low = split(field * field)
    ones = jnp.ones((8, CELLS), jnp.bfloat16)
    norms = (dot(ones, high, nt) + dot(ones, low, nt))[0:1]
    level = [jnp.full((1, lanes), flags[k].astype(jnp.float32)) for k in range(4)]
    west, east = rows[0:56], rows[56:112]
    even = place_ref[0, 0] % 2 == 0
    first_ref[0:56] = jnp.where(even, east, west)
    second_ref[0:56] = jnp.where(even, west, east)
    for ref in (first_ref, second_ref):
        ref[56:57] = level[S_]
        ref[57:58] = level[N_]
        ref[58:59] = norms
        ref[59:64] = jnp.zeros((5, lanes), jnp.float32)
    at_end = (place_ref[0, 0] == 0) | (place_ref[0, 0] == GROUP - 1)
    wrap_ref[...] = jnp.where(at_end, second_ref[...], first_ref[...])
    strips_ref[0:100] = rows[112:212]
    strips_ref[100:101] = level[E_]
    strips_ref[101:102] = level[W_]
    strips_ref[102:103] = norms
    strips_ref[103:104] = jnp.zeros((1, lanes), jnp.float32)


def second_kernel(second_ref, near_ref, out_ref):
    out_ref[0:59] = second_ref[0:59]
    out_ref[59:60] = near_ref[0:1]
    out_ref[60:61] = near_ref[LAST : LAST + 1]
    out_ref[61:62] = second_ref[58:59] + near_ref[58:59]
    out_ref[62:64] = jnp.zeros((2, out_ref.shape[1]), jnp.float32)


def across(place, other, wrap):
    return jnp.where((place == 0) | (place == GROUP - 1), wrap, other)


def third_kernel(second_ref, other_ref, wrap_ref, place_ref, out_ref):
    place = place_ref[0, 0]
    out_ref[0:1] = across(place, other_ref[0:1], wrap_ref[0:1])
    out_ref[1:2] = across(place, other_ref[LAST : LAST + 1], wrap_ref[LAST : LAST + 1])
    out_ref[2:3] = second_ref[61:62] + other_ref[61:62]
    out_ref[3:4] = wrap_ref[0:1]
    out_ref[4:5] = wrap_ref[LAST : LAST + 1]
    out_ref[5:8] = jnp.zeros((3, out_ref.shape[1]), jnp.float32)


def relay_kernel(strips_ref, second_ref, near_ref, other_ref, wrap_ref, back_ref, place_ref, out_ref, sums_ref):
    place = place_ref[0, 0]
    even = place % 2 == 0
    near = near_ref[...]
    other = across(place, other_ref[...], wrap_ref[...])
    out_ref[0:96] = strips_ref[0:96]
    row = 96
    for pack, far in (
        (jnp.where(even, near, other), jnp.where(even, back_ref[0:2], other[59:61])),
        (jnp.where(even, other, near), jnp.where(even, other[59:61], back_ref[0:2])),
    ):
        side = (row - 96) // 6
        for a, b in CORNER:
            out_ref[row : row + 1] = pack[b * SIDE + a : b * SIDE + a + 1]
            out_ref[row + 3 : row + 4] = pack[b * SIDE + LAST - a : b * SIDE + SIDE - a]
            row += 1
        row += 3
        out_ref[108 + 6 * side : 114 + 6 * side] = pack[48:54]
        own = strips_ref[96 + 2 * side : 98 + 2 * side]
        out_ref[120 + 2 * side : 122 + 2 * side] = jnp.where(pack[56:58] == 1, far, own)
    out_ref[124:126] = strips_ref[100:102]
    y = place % 4
    sums = jnp.where((y == 1) | (y == 2), second_ref[61:62] + other[61:62], back_ref[2:3])
    out_ref[126:128] = jnp.zeros((2, out_ref.shape[1]), jnp.float32)
    sums_ref[...] = jnp.broadcast_to(sums[None], sums_ref.shape)


def rate_column(diffusivity_ref, member_count):
    levels = diffusivity_ref.shape[1]
    here = lax.broadcasted_iota(jnp.int32, (levels, levels), 0)
    there = lax.broadcasted_iota(jnp.int32, (levels, levels), 1)
    column = jnp.sum(jnp.where(here == there, diffusivity_ref[...], 0.0), axis=1, keepdims=True)
    return jnp.concatenate([column] * member_count, axis=0)


def rates_kernel(diffusivity_ref, first_ref, out_ref):
    member_count = out_ref.shape[0] // diffusivity_ref.shape[1]
    out_ref[...] = jnp.broadcast_to(rate_column(diffusivity_ref, member_count), out_ref.shape)


def weighted(walks, rates):
    one, two, three = (walks[:, k * CELLS : (k + 1) * CELLS] for k in range(PASSES))
    return rates * (3.0 * one + rates * (3.0 * two + rates * three))


def own_kernel(
    field_ref, diffusivity_ref, vertical_ref, flip_ref, walks_ref, zero_ref, one_ref, edge_ref,
    base_ref, operator_ref, high_ref, low_ref,
):
    member_count, level_count, _ = field_ref.shape
    field = field_ref[...].reshape(-1, CELLS)
    rates = rate_column(diffusivity_ref, member_count)
    high, low = split(field)
    walks = dot(high, walks_ref[...]) + dot(low, walks_ref[...])
    base_ref[...] = field + weighted(walks, rates)
    flags = [flip_ref[0, k] for k in range(4)]
    flag = per_row(edge_ref[:, 0:1], flags, (edge_ref.shape[0], 1))
    flag = jnp.broadcast_to(flag, zero_ref.shape) == 1
    operator_ref[...] = jnp.where(
        flag, one_ref[...].astype(jnp.float32), zero_ref[...].astype(jnp.float32)
    ).astype(jnp.bfloat16)
    lanes = member_count * level_count
    across = jnp.concatenate([vertical_ref[...]] * member_count, axis=1)
    whole = jnp.concatenate([across] * member_count, axis=0)
    here = lax.broadcasted_iota(jnp.int32, (lanes, lanes), 0) // level_count
    there = lax.broadcasted_iota(jnp.int32, (lanes, lanes), 1) // level_count
    high, low = split(jnp.where(here == there, whole, 0.0))
    high_ref[...] = high
    low_ref[...] = low

def final_kernel(
    base_ref, operator_ref, high_ref, low_ref, arrived_ref, near_ref, other_ref, wrap_ref, back_ref,
    rates_ref, flip_ref, place_ref, perts_ref, gain_ref, term_ref,
    halo_ref,
):
    member_count, level_count, _ = perts_ref.shape
    rates = rates_ref[:, 0:1]
    place = place_ref[0, 0]
    even = place % 2 == 0
    near = near_ref[...]
    other = across(place, other_ref[...], wrap_ref[...])
    halo_ref[0:NS_ROWS] = arrived_ref[...]
    halo_ref[NS_ROWS : NS_ROWS + EW_ROWS] = jnp.where(even, near, other)
    halo_ref[NS_ROWS + EW_ROWS :] = jnp.where(even, other, near)
    for here, start, row in ((GROUP - 1, NS_ROWS, 120), (0, NS_ROWS + EW_ROWS, 122)):
        for k, flag in ((0, 57), (1, 56)):
            flagged = (halo_ref[start + flag : start + flag + 1] == 1) & (place == here)
            old = halo_ref[row + k : row + k + 1]
            halo_ref[row + k : row + k + 1] = jnp.where(flagged, back_ref[3 + k : 4 + k], old)
    halo = halo_ref[...]
    flags = [flip_ref[0, k] for k in range(4)]
    north_e = jnp.where(flags[N_] == 1, cell(LAST, 0), cell(LAST, LAST))
    north_w = jnp.where(flags[N_] == 1, cell(LAST, LAST), cell(LAST, 0))
    south_e = jnp.where(flags[S_] == 1, cell(0, 0), cell(0, LAST))
    south_w = jnp.where(flags[S_] == 1, cell(0, LAST), cell(0, 0))
    far_e = arrived_ref[124:125, 0:1] == 1
    far_w = arrived_ref[125:126, 0:1] == 1
    rows = lax.broadcasted_iota(jnp.int32, (halo.shape[0], 1), 0)
    target = jnp.full(rows.shape, -1, jnp.int32)
    for row, yes, no, far in (
        (NS_ROWS + 54, south_e, north_e, far_e),
        (NS_ROWS + 55, north_e, south_e, far_e),
        (NS_ROWS + EW_ROWS + 54, south_w, north_w, far_w),
        (NS_ROWS + EW_ROWS + 55, north_w, south_w, far_w),
    ):
        target = jnp.where(rows == row, jnp.where(far, yes, no), target)
    lane = lax.broadcasted_iota(jnp.int32, (halo.shape[0], CELLS), 1)
    corner = jnp.where(lane == target, 1.0, 0.0).astype(jnp.bfloat16)
    high, low = split(halo.T)
    operator = operator_ref[...]
    walks = dot(high, operator) + dot(low, operator)
    extra = dot(high, corner) + dot(low, corner)
    diffused = base_ref[...] + weighted(walks, rates) + rates * rates * rates * extra
    high, low = split(diffused)
    mix = dot(high_ref[...], high) + dot(high_ref[...], low) + dot(low_ref[...], high)
    total = jnp.zeros((level_count, CELLS), jnp.float32)
    for k in range(member_count):
        rows = slice(k * level_count, (k + 1) * level_count)
        total = total + perts_ref[k].astype(jnp.float32) * mix[rows]
    term_ref[...] = (gain_ref[...] * total).reshape(term_ref.shape)


def halo_rows():
    by_flag = [np.zeros((NS_ROWS + 2 * EW_ROWS, PASSES * CELLS), np.float32) for _ in range(2)]
    edge = np.full((NS_ROWS + 2 * EW_ROWS, 8), -1, np.int32)

    def put(row, zero, one=None, which=-1):
        by_flag[0][row] = WALKS[PLACE[zero]]
        by_flag[1][row] = WALKS[PLACE[one or zero]]
        edge[row] = which

    for a in range(PASSES):
        for i in range(SIDE):
            k = a * SIDE + i
            put(k, ("N", a, i))
            put(48 + k, ("S", a, i))
            put(NS_ROWS + k, ("E", a, i))
            put(NS_ROWS + EW_ROWS + k, ("W", a, i))
    for k, (a, b) in enumerate(CORNER):
        put(96 + k, ("NE", a, b), ("NW", a, b), N_)
        put(99 + k, ("SE", a, b), ("SW", a, b), S_)
        put(102 + k, ("NW", a, b), ("NE", a, b), N_)
        put(105 + k, ("SW", a, b), ("SE", a, b), S_)
        put(108 + k, ("EN", a, b), ("ES", a, b), E_)
        put(111 + k, ("ES", a, b), ("EN", a, b), E_)
        put(114 + k, ("WN", a, b), ("WS", a, b), W_)
        put(117 + k, ("WS", a, b), ("WN", a, b), W_)
    put(120, ("q", "EN"), ("q", "ES"), E_)
    put(121, ("q", "ES"), ("q", "EN"), E_)
    put(122, ("q", "WN"), ("q", "WS"), W_)
    put(123, ("q", "WS"), ("q", "WN"), W_)
    return by_flag[0], by_flag[1], edge


def vmem(count):
    return [pl.BlockSpec(memory_space=pltpu.VMEM)] * count


SMEM = pl.BlockSpec(memory_space=pltpu.SMEM)


def room(mebibytes):
    return pltpu.CompilerParams(vmem_limit_bytes=mebibytes * 2**20)


def local(control, perts, diffusivity, vertical, gain, edge_flip):
    member_count, level_count, cell_count = control.shape
    tile_count = lax.axis_size("tile")
    mem_count = lax.axis_size("mem")
    lanes = member_count * level_count
    west_table, east_table, ns_table, q_table = pack_cells()

    place = (lax.axis_index("tile") % GROUP).astype(jnp.int32).reshape(1, 1)

    def exchanged(value, pairs):
        both = [(i % tile_count, j % tile_count) for i, j in pairs]
        return lax.ppermute(value, "tile", both + [(j, i) for i, j in both])

    def swapped(value, mask):
        return lax.ppermute(value, "tile", [(i, i ^ mask) for i in range(tile_count)])

    half = tile_count // 2
    edges = range(GROUP, tile_count + 1, GROUP)
    pairs = [(i, i + 1) for i in range(0, tile_count, 2)]
    between = [(i, i + 1) for i in range(1, tile_count, 2) if (i + 1) % GROUP]

    def rows_of(count):
        return jax.ShapeDtypeStruct((count, lanes), jnp.float32)

    table = table_columns(west_table + east_table + ns_table + q_table + [(0, 0, -1)] * 4)
    first, second, wrap, strips = pl.pallas_call(
        pack_kernel,
        out_shape=[rows_of(count) for count in (EW_ROWS, EW_ROWS, EW_ROWS, 104)],
        in_specs=vmem(1) + [SMEM, SMEM] + vmem(1),
        out_specs=vmem(4),
        name="packs",
    )(control, edge_flip, place, jnp.asarray(table))
    wrap = exchanged(wrap, [(k - 1, k) for k in edges] + [(k - 2, k + 1 + half) for k in edges])
    near = exchanged(first, pairs)
    rates = pl.pallas_call(
        rates_kernel,
        out_shape=jax.ShapeDtypeStruct((lanes, 128), jnp.float32),
        in_specs=vmem(2),
        out_specs=vmem(1)[0],
        name="rates",
        compiler_params=room(4),
        cost_estimate=pl.CostEstimate(flops=4600000000, bytes_accessed=1000000, transcendentals=0),
    )(diffusivity.reshape(1, level_count), first)
    near, rates = lax.optimization_barrier((near, rates))
    second = pl.pallas_call(
        second_kernel, out_shape=rows_of(EW_ROWS), in_specs=vmem(2), out_specs=vmem(1)[0], name="second", compiler_params=room(4)
    )(second, near)
    other = exchanged(second, between)
    back = pl.pallas_call(
        third_kernel, out_shape=rows_of(8), in_specs=vmem(3) + [SMEM], out_specs=vmem(1)[0], name="third", compiler_params=room(4)
    )(second, other, wrap, place)
    back = exchanged(back, pairs)
    ns_pack, sums = pl.pallas_call(
        relay_kernel,
        out_shape=[rows_of(NS_ROWS), jax.ShapeDtypeStruct((GROUP, 1, lanes), jnp.float32)],
        in_specs=vmem(6) + [SMEM],
        out_specs=vmem(2),
        name="relay", compiler_params=room(4),
    )(strips, second, near, other, wrap, back, place)
    arrived = exchanged(ns_pack, [(i, i + half) for i in range(half)])
    control_there, ns_pack = lax.optimization_barrier((control, ns_pack))
    zero, one, edge = halo_rows()
    spread = diffusivity.reshape(1, level_count)
    wide = PASSES * cell_count
    base, operator, high, low = pl.pallas_call(
        own_kernel,
        out_shape=[
            jax.ShapeDtypeStruct((lanes, cell_count), jnp.float32),
            jax.ShapeDtypeStruct((NS_ROWS + 2 * EW_ROWS, wide), jnp.bfloat16),
            jax.ShapeDtypeStruct((lanes, lanes), jnp.bfloat16),
            jax.ShapeDtypeStruct((lanes, lanes), jnp.bfloat16),
        ],
        in_specs=vmem(3) + [SMEM] + vmem(4),
        out_specs=vmem(4),
        name="own_cells",
    )(
        control_there,
        spread,
        vertical,
        edge_flip,
        jnp.asarray(WALKS_OWN, jnp.bfloat16),
        jnp.asarray(zero, jnp.bfloat16),
        jnp.asarray(one, jnp.bfloat16),
        jnp.asarray(edge),
    )
    groups = [list(range(low_bits, tile_count, 4)) for low_bits in range(4)]
    sums = lax.all_to_all(sums, "tile", 0, 0, tiled=True, axis_index_groups=groups)
    pieces = pl.pallas_call(
        final_kernel,
        out_shape=jax.ShapeDtypeStruct((mem_count, level_count // mem_count, cell_count), jnp.float32),
        in_specs=vmem(10) + [SMEM, SMEM] + vmem(2),
        out_specs=vmem(1)[0],
        scratch_shapes=[pltpu.VMEM((NS_ROWS + 2 * EW_ROWS, lanes), jnp.float32)],
        name="localized",
                cost_estimate=pl.CostEstimate(flops=11499999999, bytes_accessed=1000000, transcendentals=0),
    )(
        base, operator, high, low, arrived, near, other, wrap, back,
        rates, edge_flip, place, perts, gain,
    )
    sums, pieces = lax.optimization_barrier((sums, pieces))
    pieces = lax.all_to_all(pieces, "mem", 0, 0, tiled=True)
    members_all = member_count * mem_count
    increment = jnp.sum(pieces, axis=0) / jnp.sqrt(jnp.float32(members_all - 1))
    norm_count = level_count * cell_count * tile_count
    sums = jnp.sum(sums[:, 0].reshape(GROUP, member_count, level_count), axis=(0, 2))
    member_cost = 0.5 * sums / norm_count
    return (increment, member_cost)


def solution(mesh):
    placed = (
        P("mem", None, "tile"),
        P("mem", None, "tile"),
        P(),
        P(),
        P(None, "tile"),
        P("tile", None),
    )
    return jax.shard_map(
        local, mesh=mesh, in_specs=placed, out_specs=(P("mem", "tile"), P("mem")), check_vma=False
    )
```
